32 devices in a mesh: beam: 2 (over core), tx: 2 (over y), ty: 4 (over z), dom: 2 (over x).
Axes of the slice: x: 2, y: 2, z: 4, core: 2. Of those that a mesh axis runs over, the one named last changes fastest.
Arguments:
- cell_row: int32 [2, 262144], P('beam', ('tx', 'ty', 'dom')), may hold values from 0 to 1022
- cell_col: int32 [2, 262144], P('beam', ('tx', 'ty', 'dom')), may hold values from 0 to 510
- weights: float32 [2, 262144], P('beam', ('tx', 'ty', 'dom')), may hold values from -6 to 6
- momenta: float32 [2, 2, 262144], P('beam', None, ('tx', 'ty', 'dom')), may hold values from -6 to 6
Outputs:
- kicked: float32 [2, 2, 262144], P('beam', None, ('tx', 'ty', 'dom'))
The draws below stay inside these ranges and needn't reach their ends.
Inputs may be any that keep to these rules, and one draw needn't show every extreme that they name: cell_row is a row within the tile of 1024 rows that holds the macroparticle, which lies on a device of that tile; its cloud also covers the next row. cell_col is a column within the tile of 512 columns that holds the macroparticle; its cloud also covers the next column.
All inputs are finite; a program needn't handle non-finite values.
Results may differ from the reference program's by a relative error of at most 0.00005.
Values sent between devices are 32-bit elements; how exact they have to be, the bound alone decides.
No kernel may reach another device: no remote copies, remote signals or barrier semaphores. Data moves between devices by JAX's collectives and lax.ppermute only.
A program may use at most 64 MiB of HBM per device.

```python
import jax
import jax.numpy as jnp
from jax import lax

GRID = 2048
P_DEV = 16384
PARTS_SIZE = 262144
TILE_ROWS = 1024
TILE_COLS = 512
N_TX = 2
N_TY = 4
N_DOM = 2


def place_ends(entries, rng, least, high):
    dims = entries.shape
    place = [jax.random.randint(jax.random.fold_in(rng, axis), (), 0, dims[axis]) for axis in range(len(dims))]
    entries = entries.at[tuple(place)].set(least)
    longest = dims.index(max(dims))
    place[longest] = (place[longest] + 1) % dims[longest]
    return entries.at[tuple(place)].set(high)


def shard_levels(key, extent, pieces, least, high):
    def one(dim, parts):
        heights = jax.random.uniform(jax.random.fold_in(jax.random.fold_in(key, 6), dim), (parts,), jnp.float32, least / len(pieces), high / len(pieces))
        return jnp.repeat(jnp.exp(heights), extent[dim] // parts).reshape((-1,) + (1,) * (len(extent) - dim - 1))

    factor_of = one(*pieces[0])
    for cut in pieces[1:]:
        factor_of = factor_of * one(*cut)
    return factor_of


def noise(rng, shape, spread, limit, shards=(), kind=jnp.bfloat16):
    factor_of = shard_levels(rng, shape, shards, -0.22, 0.18) if shards else 1.0
    entries = jax.random.normal(rng, shape, jnp.float32) * spread * factor_of
    return jnp.minimum(jnp.maximum(entries, -limit), limit).astype(kind)


def setup_inputs(seed: int = 0) -> dict:
    seeds = jax.random.split(jax.random.key(seed), 5)
    return {
        "cell_row": place_ends(jax.random.randint(seeds[0], (2, PARTS_SIZE), 0, TILE_ROWS - 1), jax.random.fold_in(seeds[0], 1), 0, (TILE_ROWS - 1) - 1).astype(jnp.int32),
        "cell_col": place_ends(jax.random.randint(seeds[1], (2, PARTS_SIZE), 0, TILE_COLS - 1), jax.random.fold_in(seeds[1], 1), 0, (TILE_COLS - 1) - 1).astype(jnp.int32),
        "weights": noise(seeds[2], (2, PARTS_SIZE), 1.0, 6.0, ((0, 2), (1, 16)), jnp.float32),
        "momenta": noise(seeds[3], (2, 2, PARTS_SIZE), 1.0, 6.0, ((0, 2), (2, 16)), jnp.float32),
    }


highest = lax.Precision.HIGHEST
kick_gain = 2.0
row_weights = (0.75, 0.25)
col_weights = (0.625, 0.375)

def basis(family, position, wavenum, points):
    period = 2 * (points + 1)
    phase_idx = (position + 1) * (wavenum + 1) % period
    angles = jnp.pi * phase_idx.astype(jnp.float32) / (points + 1)
    scaling = jnp.sqrt(jnp.float32(2.0) / (points + 1))
    if family == 'sine':
        return scaling * jnp.sin(angles)
    wavenumber = jnp.pi * (wavenum + 1).astype(jnp.float32) / (points + 1)
    return -scaling * wavenumber * jnp.cos(angles)

def eigen_value(wavenum, points):
    halfsin = jnp.sin(jnp.pi * (wavenum + 1).astype(jnp.float32) / (2 * (points + 1)))
    return 4.0 * halfsin * halfsin

def green(row_modes, col_modes, points):
    return 1.0 / (eigen_value(row_modes, points) + eigen_value(col_modes, points))

def beam_fields(charge):
    modes = jnp.arange(GRID, dtype=jnp.int32)
    sine = basis('sine', modes[:, None], modes[None, :], GRID)
    slope = basis('slope', modes[:, None], modes[None, :], GRID)
    spectrum = jnp.dot(jnp.dot(sine, charge, precision=highest), sine, precision=highest)
    potential_hat = green(modes[:, None], modes[None, :], GRID) * spectrum
    along = jnp.dot(potential_hat, sine, precision=highest)
    across = jnp.dot(potential_hat, slope.T, precision=highest)
    field_x = jnp.dot(slope, along, precision=highest)
    field_y = jnp.dot(sine, across, precision=highest)
    return (field_x, field_y)

def global_cells(local_row, local_col):
    particle = jnp.arange(local_row.shape[0], dtype=jnp.int32)
    device = particle // P_DEV
    tile_x = device // (N_TY * N_DOM)
    tile_y = device // N_DOM % N_TY
    return (tile_x * (GRID // N_TX) + local_row, tile_y * (GRID // N_TY) + local_col)

def deposit(grid_row, grid_col, charges):
    charge = jnp.zeros((GRID, GRID), jnp.float32)
    for row_off in range(2):
        for col_off in range(2):
            amount = row_weights[row_off] * (col_weights[col_off] * charges)
            charge = charge.at[grid_row + row_off, grid_col + col_off].add(amount)
    return charge

def sample(field, grid_row, grid_col):
    result = jnp.zeros(grid_row.shape, jnp.float32)
    for row_off in range(2):
        for col_off in range(2):
            result = result + row_weights[row_off] * col_weights[col_off] * field[grid_row + row_off, grid_col + col_off]
    return result

def reference(cell_row, cell_col, weights, momenta):
    cells = [global_cells(cell_row[beam_no], cell_col[beam_no]) for beam_no in range(2)]
    fields = [beam_fields(deposit(cells[beam_no][0], cells[beam_no][1], weights[beam_no])) for beam_no in range(2)]
    kicks = []
    for beam_no in range(2):
        field_x, field_y = fields[1 - beam_no]
        grid_row, grid_col = cells[beam_no]
        kicks.append(jnp.stack([sample(field_x, grid_row, grid_col), sample(field_y, grid_row, grid_col)]))
    return momenta + kick_gain * jnp.stack(kicks)
```

```python
import functools

import jax
import jax.numpy as jnp
import ml_dtypes
import numpy as np
from jax import lax
from jax.experimental import pallas as pl
from jax.experimental.pallas import tpu as pltpu
from jax.sharding import Mesh
from jax.sharding import PartitionSpec as P

GRID = 2048
HALF = GRID // 2
kick_gain = 2.0
block = 512
window = 256
cube = ("q", "tx", "lo", "dom")
vmem_limit = 48 * 1024 * 1024


def split_table(values):
    high = values.astype(ml_dtypes.bfloat16)
    low = (values - high.astype(np.float64)).astype(ml_dtypes.bfloat16)
    return (high, low)


@functools.lru_cache(maxsize=None)
def basis_tables():
    points = GRID + 1
    position = np.arange(HALF + 1)[:, None] + 1
    wave = np.arange(GRID)[None, :] + 1
    angles = np.pi * ((position * wave) % (2 * points)) / points
    scaling = np.sqrt(2.0 / points)
    sine = scaling * np.sin(angles)
    slope = -scaling * (np.pi * wave / points) * np.cos(angles)
    return (sine[:, 0::2], sine[:, 1::2], slope[:, 0::2], slope[:, 1::2])


def split(values):
    high = lax.reduce_precision(values, 8, 7)
    return (high.astype(jnp.bfloat16), (values - high).astype(jnp.bfloat16))


def dot(left, right, dims):
    return lax.dot_general(left, right, (dims, ((), ())), preferred_element_type=jnp.float32)


def table_left(table, values, contract):
    high, low = split(values)
    width = values.shape[1]
    both = dot(table[0], jnp.concatenate([high, low], 1), ((contract,), (0,)))
    return both[:, :width] + both[:, width:] + dot(table[1], high, ((contract,), (0,)))


def table_right(values, table, contract):
    high, low = split(values)
    rows = values.shape[0]
    both = dot(jnp.concatenate([high, low], 0), table[0], ((1,), (contract,)))
    return both[:rows] + both[rows:] + dot(high, table[1], ((1,), (contract,)))


def pair_weights(index, first, second, shape):
    rows = lax.broadcasted_iota(jnp.int32, shape, 0)
    return jnp.where(rows == index, first, jnp.where(rows == index + 1, second, 0.0))


def deposit_kernel(strips, halves, meta, scalars, weights, lists, charge):
    pad_cols = charge.shape[1]
    blocks = lists.shape[2] // block
    charge[...] = jnp.zeros_like(charge)

    def one_block(turn, carry):
        which = turn // blocks
        offset = pl.multiple_of((turn % blocks) * block, block)
        here = pl.ds(offset, block)
        half = jnp.where(which >= halves, 1, 0)
        start = meta[0, turn]

        def one_window(step, carry):
            at = pl.multiple_of(start + step * window, 128)
            row = lists[which, 0:1, here].astype(jnp.int32) - at
            col = lists[which, 1:2, here].astype(jnp.int32) - scalars[0]
            col = jnp.where((col >= 0) & (col < strips), col, -10)
            amount = lists[which, 2:3, here]
            near, far = (weights[which, 2] * amount, weights[which, 3] * amount)
            near_high = near.astype(jnp.bfloat16).astype(jnp.float32)
            far_high = far.astype(jnp.bfloat16).astype(jnp.float32)
            cols = jnp.concatenate(
                [
                    pair_weights(col, near_high, far_high, (pad_cols, block)),
                    pair_weights(col, near - near_high, far - far_high, (pad_cols, block)),
                ],
                0,
            ).astype(jnp.bfloat16)
            rows = pair_weights(row, weights[which, 0], weights[which, 1], (window, block)).astype(jnp.bfloat16)
            both = dot(cols, rows, ((1,), (1,)))
            charge[half, :, pl.ds(at, window)] += both[:pad_cols] + both[pad_cols:]
            return carry

        return lax.fori_loop(0, meta[1, turn], one_window, carry)

    lax.fori_loop(0, lists.shape[0] * blocks, one_block, 0)


def sample_kernel(strips, halves, meta, scalars, weights, lists, field_high, field_low, kicks):
    pad_cols = field_high.shape[1] // 2
    blocks = lists.shape[2] // block
    kicks[...] = jnp.zeros_like(kicks)

    def one_block(turn, carry):
        which = turn // blocks
        offset = pl.multiple_of((turn % blocks) * block, block)
        here = pl.ds(offset, block)
        half = jnp.where(which >= halves, 1, 0)
        start = meta[0, turn]

        def one_window(step, carry):
            at = pl.multiple_of(start + step * window, 128)
            row = lists[which, 0:1, here].astype(jnp.int32) - at
            col = lists[which, 1:2, here].astype(jnp.int32) - scalars[0]
            col = jnp.where((col >= 0) & (col < strips), col, -10)
            rows = pair_weights(row, weights[which, 0], weights[which, 1], (window, block)).astype(jnp.bfloat16)
            fields = jnp.concatenate(
                [field_high[half, :, pl.ds(at, window)], field_low[half, :, pl.ds(at, window)]], 1
            )
            near = dot(fields, jnp.concatenate([rows, rows], 0), ((1,), (0,)))
            cols = pair_weights(col, weights[which, 2], weights[which, 3], (pad_cols, block))
            kicks[which, 0:1, here] += jnp.sum(near[:pad_cols] * cols, axis=0, keepdims=True)
            kicks[which, 1:2, here] += jnp.sum(near[pad_cols:] * cols, axis=0, keepdims=True)
            return carry

        return lax.fori_loop(0, meta[1, turn], one_window, carry)

    lax.fori_loop(0, lists.shape[0] * blocks, one_block, 0)


def window_meta(row, col, strip_start, strips):
    shape = (row.shape[0], row.shape[1] // block, block)
    row, col = (row.reshape(shape), col.reshape(shape))
    inside = (col >= strip_start) & (col < strip_start + strips)
    least = jnp.min(jnp.where(inside, row, 2.0 * GRID), axis=2).astype(jnp.int32)
    most = jnp.max(jnp.where(inside, row, -1.0), axis=2).astype(jnp.int32)
    start = least // 128 * 128
    count = jnp.where(most < 0, 0, (most + 1 - start) // window + 1)
    return jnp.stack([jnp.where(most < 0, 0, start).reshape(-1), count.reshape(-1)])


def shards(cell_row, cell_col, weights, momenta):
    n_tx, n_lo, n_dom = (lax.axis_size(name) for name in ("tx", "lo", "dom"))
    tile_rows = GRID // n_tx
    tile_cols = HALF // n_lo
    lists = n_tx * n_dom
    strips = tile_cols // lists
    pad_cols = strips + 8
    devices = 2 * n_lo * lists
    modes = GRID // devices
    count = cell_row.shape[1]
    q, hi, lo, tx, dom = (lax.axis_index(name) for name in ("q", "hi", "lo", "tx", "dom"))

    row, col, amount = (cell_row[0], cell_col[0], weights[0])
    row = jnp.where(tx >= n_tx // 2, (n_tx - 1 - tx) * tile_rows + (tile_rows - 2) - row, tx * tile_rows + row)
    col = jnp.where(hi == 1, tile_cols - 2 - col, col)
    key = (col // strips * HALF + row) * strips + col % strips
    key, amount, order = lax.sort((key, amount, lax.iota(jnp.int32, count)), num_keys=1, is_stable=False)
    row = (key // strips) % HALF
    col = key // (strips * HALF) * strips + key % strips
    row, col = (row.astype(jnp.float32), col.astype(jnp.float32))

    own_route = [(b * 2 + t, t * 2 + b) for b in range(2) for t in range(2)]
    other_route = [(b * 2 + t, t * 2 + 1 - b) for b in range(2) for t in range(2)]
    back_route = [(there, here) for here, there in other_route]
    own = lax.ppermute(jnp.stack([row, col, amount]), ("q", "hi"), own_route)
    own = lax.all_gather(own, ("tx", "dom"), axis=0)
    other = lax.ppermute(jnp.stack([row, col]), ("q", "hi"), other_route)
    other = lax.all_gather(other, ("tx", "dom"), axis=0)

    strip_start = (tx * n_dom + dom) * strips
    flipped_rows = jnp.arange(lists)[:, None] // n_dom >= n_tx // 2
    row_pair = jnp.where(flipped_rows, jnp.array([[0.25, 0.75]]), jnp.array([[0.75, 0.25]]))
    col_pair = jnp.where(q == 1, jnp.array([[0.375, 0.625]]), jnp.array([[0.625, 0.375]]))
    pairs = jnp.concatenate([row_pair, jnp.broadcast_to(col_pair, (lists, 2))], 1).astype(jnp.float32)
    scalars = strip_start.astype(jnp.int32).reshape(1)
    smem, vmem = (pl.BlockSpec(memory_space=pltpu.SMEM), pl.BlockSpec(memory_space=pltpu.VMEM))
    params = pltpu.CompilerParams(vmem_limit_bytes=vmem_limit)

    own_meta = window_meta(own[:, 0], own[:, 1], strip_start.astype(jnp.float32), strips)
    charge = pl.pallas_call(
        functools.partial(deposit_kernel, strips, lists // 2),
        out_shape=jax.ShapeDtypeStruct((2, pad_cols, HALF + window), jnp.float32),
        in_specs=[smem, smem, smem, vmem],
        out_specs=vmem,
        compiler_params=params,
        name="deposit",
    )(own_meta, scalars, pairs, own)[:, :, :HALF]

    sine_even, sine_odd, slope_even, slope_odd = basis_tables()
    sine_e, sine_o, slope_e, slope_o = (
        tuple(jnp.asarray(part) for part in split_table(table[:HALF])) for table in basis_tables()
    )
    starts = np.array([b * tile_cols + (a * n_dom + c) * strips for a in range(n_tx) for b in range(n_lo) for c in range(n_dom)])
    offsets = np.arange(pad_cols)
    picked = np.where(offsets <= strips, starts[:, None] + offsets, 0).reshape(-1)
    used = np.broadcast_to(offsets <= strips, (len(starts), pad_cols)).reshape(-1, 1)
    strip_sine_e, strip_sine_o, strip_slope_e, strip_slope_o = (
        tuple(jnp.asarray(part) for part in split_table(table[picked] * used)) for table in basis_tables()
    )

    even = table_right(charge[0] + charge[1], sine_e, 0)
    odd = table_right(charge[0] - charge[1], sine_o, 0)
    by_mode = jnp.concatenate([even, odd], 1).reshape(pad_cols, devices, modes).transpose(1, 0, 2)
    by_mode = lax.all_to_all(by_mode, cube, 0, 0, tiled=True)

    def flip(part):
        return part.reshape(n_tx, n_lo, n_dom, pad_cols, modes)[:, ::-1].reshape(devices // 2, pad_cols, modes)

    near, far = (by_mode[: devices // 2], flip(by_mode[devices // 2 :]))
    folded = (devices // 2 * pad_cols, modes)
    spectrum_e = table_left(strip_sine_e, (near + far).reshape(folded), 0)
    spectrum_o = table_left(strip_sine_o, (near - far).reshape(folded), 0)
    angles = np.pi * (np.arange(GRID) + 1) / (2 * (GRID + 1))
    lam = (4.0 * np.sin(angles) ** 2).astype(np.float32)
    lam_e, lam_o = (lam[0::2], lam[1::2])
    lam_k = lax.dynamic_slice_in_dim(jnp.asarray(np.concatenate([lam_e, lam_o])), lax.axis_index(cube) * modes, modes)
    hat_e = spectrum_e * (1.0 / (lam_e[:, None] + lam_k[None, :]))
    hat_o = spectrum_o * (1.0 / (lam_o[:, None] + lam_k[None, :]))
    shape = (devices // 2, pad_cols, modes)
    along_e = table_left(strip_sine_e, hat_e, 1).reshape(shape)
    along_o = table_left(strip_sine_o, hat_o, 1).reshape(shape)
    across_e = table_left(strip_slope_e, hat_e, 1).reshape(shape)
    across_o = table_left(strip_slope_o, hat_o, 1).reshape(shape)
    halves = jnp.concatenate(
        [
            jnp.stack([along_e + along_o, across_e + across_o], 1),
            jnp.stack([flip(along_e - along_o), flip(across_o - across_e)], 1),
        ],
        0,
    )
    halves = lax.all_to_all(halves, cube, 0, 0, tiled=True)

    halves = halves.transpose(1, 2, 0, 3).reshape(2, pad_cols, GRID)
    x_e = table_right(halves[0, :, :HALF], slope_e, 1)
    x_o = table_right(halves[0, :, HALF:], slope_o, 1)
    y_e = table_right(halves[1, :, :HALF], sine_e, 1)
    y_o = table_right(halves[1, :, HALF:], sine_o, 1)
    field = jnp.stack([jnp.concatenate([x_e + x_o, y_e + y_o], 0), jnp.concatenate([x_o - x_e, y_e - y_o], 0)])
    field = jnp.pad(field, ((0, 0), (0, 0), (0, window)))
    field_high, field_low = split(field)

    other_meta = window_meta(other[:, 0], other[:, 1], strip_start.astype(jnp.float32), strips)
    kicks = pl.pallas_call(
        functools.partial(sample_kernel, strips, lists // 2),
        out_shape=jax.ShapeDtypeStruct((lists, 2, count), jnp.float32),
        in_specs=[smem, smem, smem, vmem, vmem, vmem],
        out_specs=vmem,
        compiler_params=params,
        name="sample",
    )(other_meta, scalars, pairs, other, field_high, field_low)
    kicks = jnp.sum(lax.all_to_all(kicks, ("tx", "dom"), 0, 0, tiled=True), axis=0)
    kicks = lax.ppermute(kicks, ("q", "hi"), back_route)
    _, kick_x, kick_y = lax.sort((order, kicks[0], kicks[1]), num_keys=1, is_stable=False)
    return momenta + kick_gain * jnp.stack([kick_x, kick_y])[None]


def solution(mesh):
    n_beam, n_tx, n_ty, n_dom = (mesh.shape[name] for name in ("beam", "tx", "ty", "dom"))
    split_mesh = Mesh(mesh.devices.reshape(n_beam, n_tx, 2, n_ty // 2, n_dom), ("q", "tx", "hi", "lo", "dom"))
    where = ("tx", "hi", "lo", "dom")
    placed = (P("q", where), P("q", where), P("q", where), P("q", None, where))
    return jax.shard_map(
        shards,
        mesh=split_mesh,
        in_specs=placed,
        out_specs=P("q", None, where),
        check_vma=False,
    )
```

```python
import functools

import jax
import jax.numpy as jnp
import ml_dtypes
import numpy as np
from jax import lax
from jax.experimental import pallas as pl
from jax.experimental.pallas import tpu as pltpu
from jax.sharding import Mesh
from jax.sharding import PartitionSpec as P

GRID = 2048
HALF = GRID // 2
kick_gain = 2.0
block = 512
window = 256
pieces = 4
piece_rows = HALF // pieces
cube = ("q", "tx", "lo", "dom")
vmem_limit = 48 * 1024 * 1024


def split_table(values):
    high = values.astype(ml_dtypes.bfloat16)
    low = (values - high.astype(np.float64)).astype(ml_dtypes.bfloat16)
    return (high, low)


@functools.lru_cache(maxsize=None)
def basis_tables():
    points = GRID + 1
    position = np.arange(HALF)[:, None] + 1
    wave = np.arange(GRID)[None, :] + 1
    angles = np.pi * ((position * wave) % (2 * points)) / points
    scaling = np.sqrt(2.0 / points)
    sine = scaling * np.sin(angles)
    slope = -scaling * (np.pi * wave / points) * np.cos(angles)
    return (sine[:, 0::2], sine[:, 1::2], slope[:, 0::2], slope[:, 1::2])


def split(values):
    high = lax.reduce_precision(values, 8, 7)
    return (high.astype(jnp.bfloat16), (values - high).astype(jnp.bfloat16))


def dot(left, right, dims):
    return lax.dot_general(left, right, (dims, ((), ())), preferred_element_type=jnp.float32)


def table_left(table, values, contract):
    high, low = split(values)
    width = values.shape[1]
    both = dot(table[0], jnp.concatenate([high, low], 1), ((contract,), (0,)))
    return both[:, :width] + both[:, width:] + dot(table[1], high, ((contract,), (0,)))


def table_right(values, table, contract):
    high, low = split(values)
    rows = values.shape[0]
    both = dot(jnp.concatenate([high, low], 0), table[0], ((1,), (contract,)))
    return both[:rows] + both[rows:] + dot(high, table[1], ((1,), (contract,)))


def pair_weights(index, first, second, rows):
    shape = (rows, index.shape[1])
    at = lax.broadcasted_iota(jnp.int32, shape, 0).astype(jnp.float32).astype(index.dtype)
    one, zero = (jnp.ones((), index.dtype), jnp.zeros((), first.dtype))
    return jnp.where(at == index, first, jnp.where(at == index + one, second, zero))


def short(values):
    return values.astype(jnp.float32).astype(jnp.bfloat16)


def dot_parts(table_high, table_low, values, dims):
    high = values.astype(jnp.bfloat16).astype(jnp.float32)
    rows = values.shape[0]
    both = dot(jnp.concatenate([high, values - high], 0).astype(jnp.bfloat16), table_high, dims)
    return both[:rows] + both[rows:] + dot(high.astype(jnp.bfloat16), table_low, dims)


def windows(strips, start, first, last, which, turn):
    first_row, first_col = (first[which, 0, turn], first[which, 1, turn])
    last_row, last_col = (last[which, 0, turn], last[which, 1, turn])
    least = jnp.where(first_col >= start, first_row, 0) // 128 * 128
    most = jnp.where(last_col < start + strips, last_row, HALF - 2)
    return (least, (most + 1 - least) // window + 1)


def each_window(strips, scalars, first, last, group, item):
    start = scalars[0]

    def bounds(turn, found):
        return tuple(
            (
                low + jnp.where(last[which, 1, turn] < start, 1, 0),
                high + jnp.where(first[which, 1, turn] < start + strips, 1, 0),
            )
            for which, (low, high) in zip(group, found, strict=True)
        )

    found = lax.fori_loop(0, first.shape[2], bounds, tuple((0, 0) for _ in group))
    turns = functools.reduce(jnp.maximum, [high - low for low, high in found])

    def one_turn(step, carry):
        more = []
        for place, (which, (low, high)) in enumerate(zip(group, found, strict=True)):
            valid = low + step < high
            turn = jnp.minimum(low + step, first.shape[2] - 1)
            at, count = windows(strips, start, first, last, which, turn)
            item(place, which, turn, pl.multiple_of(at, 128), valid)
            more.append((place, which, turn, at, jnp.where(valid, count, 0)))
        for place, which, turn, at, count in more:

            def one_window(extra, carry, place=place, which=which, turn=turn, at=at):
                item(place, which, turn, pl.multiple_of(at + extra * window, 128), True)
                return carry

            lax.fori_loop(1, count, one_window, 0)
        return carry

    lax.fori_loop(0, turns, one_turn, 0)


def cells_of(strips, scalars, lists, which, here, at, valid):
    row = lists[which, 0:1, here].astype(jnp.int32) - at
    row = jnp.where((row >= -1) & (row < window) & valid, row, -10)
    col = lists[which, 1:2, here].astype(jnp.int32) - scalars[0]
    col = jnp.where((col >= 0) & (col < strips), col, -10)
    return (row, col)


def groups_of(count):
    return [tuple(range(first, min(first + 4, count))) for first in range(0, count, 4)]


def deposit_body(strips, scalars, first, last, weights, lists, charge, parts):
    pad_cols = charge.shape[1]
    tall = -(-pad_cols // 16) * 16
    count = lists.shape[0]
    for part in parts:
        part[...] = jnp.zeros_like(part)

    def half_of(which):
        return which // (count // 2)

    def item(place, which, turn, at, valid):
        here = pl.ds(pl.multiple_of(turn * block, block), block)
        row, col = cells_of(strips, scalars, lists, which, here, at, valid)
        amount = lists[which, 2:3, here]
        near, far = (weights[which, 2] * amount, weights[which, 3] * amount)
        near_high, far_high = (near.astype(jnp.bfloat16), far.astype(jnp.bfloat16))
        near_low = (near - near_high.astype(jnp.float32)).astype(jnp.bfloat16)
        far_low = (far - far_high.astype(jnp.float32)).astype(jnp.bfloat16)
        col = short(col)
        cols = jnp.concatenate(
            [pair_weights(col, near_high, far_high, tall), pair_weights(col, near_low, far_low, tall)], 0
        )
        rows = pair_weights(short(row), short(weights[which, 0]), short(weights[which, 1]), window)
        both = dot(cols, rows, ((1,), (1,)))
        half = half_of(which) if count > 4 else 0
        parts[place][half, :, pl.ds(at, window)] += both[:pad_cols] + both[tall : tall + pad_cols]

    for group in groups_of(count):
        each_window(strips, scalars, first, last, group, item)
    for half in range(2):
        if count > 4:
            used = [part[half] for part in parts]
        else:
            used = [part[0] for which, part in enumerate(parts) if half_of(which) == half]
        charge[half] = functools.reduce(jnp.add, used)


def deposit_parts(count, charge_shape):
    return [pltpu.VMEM((2 if count > 4 else 1, *charge_shape[1:]), jnp.float32)] * min(count, 4)


def sample_body(strips, scalars, first, last, weights, lists, field_high, field_low, kicks, begin):
    pad_cols = field_high.shape[1] // 2
    for kick in kicks:
        kick[...] = jnp.zeros_like(kick)

    def item(place, which, turn, at, valid):
        here = pl.ds(pl.multiple_of(turn * block, block), block)
        half = scalars[1 + which]
        kick = kicks[which - begin]
        row, col = cells_of(strips, scalars, lists, which, here, at, valid)
        rows = pair_weights(short(row), short(weights[which, 0]), short(weights[which, 1]), window)
        fields = jnp.concatenate([field_high[half, :, pl.ds(at, window)], field_low[half, :, pl.ds(at, window)]], 1)
        near = dot(fields, jnp.concatenate([rows, rows], 0), ((1,), (0,)))
        cols = pair_weights(col.astype(jnp.float32), weights[which, 2], weights[which, 3], pad_cols)
        kick[0:1, here] += jnp.sum(near[:pad_cols] * cols, axis=0, keepdims=True)
        kick[1:2, here] += jnp.sum(near[pad_cols:] * cols, axis=0, keepdims=True)

    for group in groups_of(len(kicks)):
        group = tuple(begin + which for which in group)
        each_window(strips, scalars, first, last, group, item)


def fetch(stored, tables, arrived, order):
    copies = {}
    for number, (part, piece) in enumerate(order):
        rows = pl.ds(piece * piece_rows, piece_rows)
        copies[part, piece] = pltpu.make_async_copy(stored.at[part, rows], tables.at[part, rows], arrived.at[number])
        copies[part, piece].start()

    def table(part, piece):
        copies[part, piece].wait()
        return tables[part, piece * piece_rows : (piece + 1) * piece_rows]

    return table


def modes_kernel(strips, scalars, first, last, weights, lists, stored, by_mode, charge, tables, arrived, *parts):
    table = fetch(stored, tables, arrived, [(part, piece) for part in range(4) for piece in range(pieces)])
    deposit_body(strips, scalars, first, last, weights, lists, charge, parts)
    devices, _, modes = by_mode.shape
    near, far = (charge[0, :, :HALF], charge[1, :, :HALF])
    for parity, part in enumerate((near + far, near - far)):
        high, low = (jnp.concatenate([table(2 * parity + i, piece) for piece in range(pieces)], 0) for i in range(2))
        done = dot_parts(high, low, part, ((1,), (0,)))
        for turn in range(devices // 2):
            by_mode[parity * (devices // 2) + turn] = done[:, turn * modes : (turn + 1) * modes]


def columns_kernel(order, flipped, per_tile, strips, by_mode, lam, lam_mine, stored, halves, tables, arrived, back_x, back_y, sent):
    forward = [(2 * parity + i, piece) for parity in range(2) for piece in range(pieces) for i in range(2)]
    backward = [(part, piece) for piece in range(pieces) for part in range(4, 8)]
    table = fetch(stored, tables, arrived, forward + backward)
    modes = by_mode.shape[2]
    near, far = ([], [])
    for place in range(len(order)):
        pair = []
        for here, before in ((order, 0), (flipped, len(order))):
            body = by_mode[before + here[place], :strips]
            if place % per_tile:
                halo = by_mode[before + here[place - 1], strips:]
                body = jnp.concatenate([body[:8] + halo, body[8:]], 0)
            pair.append(body)
        near.append(pair[0] + pair[1])
        far.append(pair[0] - pair[1])
    hats = []
    for parity, part in enumerate((near, far)):
        part = jnp.concatenate(part, 0).T
        spectrum = 0.0
        for piece in range(pieces):
            high, low = (table(2 * parity + i, piece) for i in range(2))
            spectrum += dot_parts(high, low, part[:, piece * piece_rows : (piece + 1) * piece_rows], ((1,), (0,)))
        hat = (spectrum * (1.0 / (lam[parity : parity + 1, :] + lam_mine[...]))).T
        high = hat.astype(jnp.bfloat16)
        hats.append((high, jnp.concatenate([high, (hat - high.astype(jnp.float32)).astype(jnp.bfloat16)], 1)))

    def back(table_high, table_low, parity):
        high, both = hats[parity]
        done = dot(table_high, both, ((1,), (0,)))
        return done[:, :modes] + done[:, modes:] + dot(table_low, high, ((1,), (0,)))

    copies = []
    for component, (outgoing, sign) in enumerate(((back_x, 1), (back_y, -1))):
        for piece in range(pieces):
            if component == 0:
                rows = slice(piece * piece_rows, (piece + 1) * piece_rows)
                parts = [tables[i, rows] for i in range(4)]
            else:
                parts = [table(4 + i, piece) for i in range(4)]
            even, odd = (back(parts[0], parts[1], 0), back(parts[2], parts[3], 1))
            for before, whose, value in (
                (0, order, even + odd),
                (len(order), flipped, even - odd if sign == 1 else odd - even),
            ):
                for turn in range(piece_rows // strips):
                    place = piece * piece_rows // strips + turn
                    mine = value[turn * strips : (turn + 1) * strips]
                    outgoing[before + whose[place], :strips] = mine
                    if place % per_tile:
                        outgoing[before + whose[place - 1], strips:] = mine[:8]
                    if place % per_tile == per_tile - 1:
                        outgoing[before + whose[place], strips:] = jnp.zeros_like(mine[:8])
        copies.append(pltpu.make_async_copy(outgoing, halves.at[:, component], sent.at[component]))
        copies[-1].start()
    for copy in copies:
        copy.wait()


def kicks_kernel(strips, scalars, first, last, weights, lists, halves, stored, *refs):
    kicks, (field_high, field_low, tables, arrived) = (refs[:-4], refs[-4:])
    order = [(part, piece) for parts in ((4, 5, 6, 7), (0, 1, 2, 3)) for piece in range(pieces) for part in parts]
    table = fetch(stored, tables, arrived, order)
    devices, _, pad_cols, _ = halves.shape
    wide = 2 * pad_cols
    fields = {}
    for component, (which, sign) in enumerate(((4, -1), (0, 1))):
        sides = []
        for start in (0, devices // 2):
            part = jnp.concatenate([halves[start + turn, component] for turn in range(devices // 2)], 1)
            high = part.astype(jnp.bfloat16)
            low = part - high.astype(jnp.float32)
            sides.append((jnp.concatenate([high.astype(jnp.float32), low], 0).astype(jnp.bfloat16), high))
        for piece in range(pieces):
            pair = []
            for parity, (both, high) in enumerate(sides):
                table_high, table_low = (table(which + 2 * parity + i, piece) for i in range(2))
                done = dot(both, table_high, ((1,), (1,)))
                pair.append(done[:pad_cols] + done[pad_cols:] + dot(high, table_low, ((1,), (1,))))
            even, odd = pair
            fields[component, piece] = (even + odd, even - odd if sign == 1 else odd - even)
    for half in range(2):
        for piece in range(pieces):
            here = slice(piece * piece_rows, (piece + 1) * piece_rows)
            value = jnp.concatenate([fields[component, piece][half] for component in range(2)], 0)
            high = value.astype(jnp.bfloat16)
            field_high[half, :, here] = high
            field_low[half, :, here] = (value - high.astype(jnp.float32)).astype(jnp.bfloat16)
        beyond = jnp.zeros((wide, window), jnp.bfloat16)
        field_high[half, :, HALF:] = beyond
        field_low[half, :, HALF:] = beyond
    sample_body(strips, scalars, first, last, weights, lists, field_high, field_low, kicks, 0)


def block_ends(lists):
    ends = (lists[:, :2, 0::block], lists[:, :2, block - 1 :: block])
    return tuple(end.astype(jnp.int32) for end in ends)


def deposit_alone(strips, scalars, first, last, weights, lists, charge, *parts):
    deposit_body(strips, scalars, first, last, weights, lists, charge, parts)


def sample_alone(strips, begin, scalars, first, last, weights, lists, field_high, field_low, *kicks):
    sample_body(strips, scalars, first, last, weights, lists, field_high, field_low, kicks, begin)


def shifted(n_tx, n_dom, shift):
    return [
        ((a + shift[0]) % n_tx * n_dom + (c + shift[1]) % n_dom, a * n_dom + c) for a in range(n_tx) for c in range(n_dom)
    ]


def returned(route, n_tx, n_dom, shift):
    pairs = []
    for there, here in route:
        for a in range(n_tx):
            for c in range(n_dom):
                target = ((there // 2 * n_tx + (a + shift[0]) % n_tx) * 2 + there % 2) * n_dom + (c + shift[1]) % n_dom
                pairs.append((((here // 2 * n_tx + a) * 2 + here % 2) * n_dom + c, target))
    return pairs


def general(to_deposit, to_sample, tables, lam_e, lam_o, lam_k, sizes, charge_shape, kick_shape):
    n_tx, n_lo, n_dom = sizes
    devices = 2 * n_tx * n_lo * n_dom
    modes = GRID // devices
    tile_cols = HALF // n_lo
    strips = tile_cols // (n_tx * n_dom)
    pad_cols = charge_shape[1]
    smem, vmem = (pl.BlockSpec(memory_space=pltpu.SMEM), pl.BlockSpec(memory_space=pltpu.VMEM))
    params = pltpu.CompilerParams(vmem_limit_bytes=vmem_limit)
    sine_e, sine_o, slope_e, slope_o = tables
    starts = np.array([b * tile_cols + (a * n_dom + c) * strips for a in range(n_tx) for b in range(n_lo) for c in range(n_dom)])
    offsets = np.arange(pad_cols)
    columns = starts[:, None] + offsets
    kept = (offsets <= strips) & (columns < HALF)
    picked = np.where(kept, columns, 0).reshape(-1)
    used = kept.reshape(-1, 1)
    strip_sine_e, strip_sine_o, strip_slope_e, strip_slope_o = (
        tuple(jnp.asarray(part) for part in split_table(table[picked] * used)) for table in basis_tables()
    )

    charge = pl.pallas_call(
        functools.partial(deposit_alone, strips),
        out_shape=jax.ShapeDtypeStruct(charge_shape, jnp.float32),
        in_specs=[smem] * 4 + [vmem],
        out_specs=vmem,
        scratch_shapes=deposit_parts(n_tx * n_dom, charge_shape),
        compiler_params=params,
        name="deposit",
    )(*to_deposit)[:, :, :HALF]

    even = table_right(charge[0] + charge[1], sine_e, 0)
    odd = table_right(charge[0] - charge[1], sine_o, 0)
    by_mode = jnp.concatenate([even, odd], 1).reshape(pad_cols, devices, modes).transpose(1, 0, 2)
    by_mode = lax.all_to_all(by_mode, cube, 0, 0, tiled=True)

    def flip(part):
        return part.reshape(n_tx, n_lo, n_dom, pad_cols, modes)[:, ::-1].reshape(devices // 2, pad_cols, modes)

    near, far = (by_mode[: devices // 2], flip(by_mode[devices // 2 :]))
    folded = (devices // 2 * pad_cols, modes)
    spectrum_e = table_left(strip_sine_e, (near + far).reshape(folded), 0)
    spectrum_o = table_left(strip_sine_o, (near - far).reshape(folded), 0)
    hat_e = spectrum_e * (1.0 / (lam_e[:, None] + lam_k[None, :]))
    hat_o = spectrum_o * (1.0 / (lam_o[:, None] + lam_k[None, :]))
    shape = (devices // 2, pad_cols, modes)
    along_e = table_left(strip_sine_e, hat_e, 1).reshape(shape)
    along_o = table_left(strip_sine_o, hat_o, 1).reshape(shape)
    across_e = table_left(strip_slope_e, hat_e, 1).reshape(shape)
    across_o = table_left(strip_slope_o, hat_o, 1).reshape(shape)
    halves = jnp.concatenate(
        [
            jnp.stack([along_e + along_o, across_e + across_o], 1),
            jnp.stack([flip(along_e - along_o), flip(across_o - across_e)], 1),
        ],
        0,
    )
    halves = lax.all_to_all(halves, cube, 0, 0, tiled=True)

    halves = halves.transpose(1, 2, 0, 3).reshape(2, pad_cols, GRID)
    x_e = table_right(halves[0, :, :HALF], slope_e, 1)
    x_o = table_right(halves[0, :, HALF:], slope_o, 1)
    y_e = table_right(halves[1, :, :HALF], sine_e, 1)
    y_o = table_right(halves[1, :, HALF:], sine_o, 1)
    field = jnp.stack([jnp.concatenate([x_e + x_o, y_e + y_o], 0), jnp.concatenate([x_o - x_e, y_e - y_o], 0)])
    field = jnp.pad(field, ((0, 0), (0, 0), (0, window)))
    field_high, field_low = split(field)

    return pl.pallas_call(
        functools.partial(sample_alone, strips, 0),
        out_shape=[kick_shape] * (n_tx * n_dom),
        in_specs=[smem] * 4 + [vmem] * 3,
        out_specs=[vmem] * (n_tx * n_dom),
        compiler_params=params,
        name="sample",
    )(*to_sample, field_high, field_low)


def shards(cell_row, cell_col, weights, momenta):
    n_tx, n_lo, n_dom = (lax.axis_size(name) for name in ("tx", "lo", "dom"))
    tile_rows = GRID // n_tx
    tile_cols = HALF // n_lo
    lists = n_tx * n_dom
    strips = tile_cols // lists
    pad_cols = strips + 8
    devices = 2 * n_lo * lists
    modes = GRID // devices
    count = cell_row.shape[1]
    q, hi, lo, tx, dom = (lax.axis_index(name) for name in ("q", "hi", "lo", "tx", "dom"))

    row, col, amount = (cell_row[0], cell_col[0], weights[0])
    row = jnp.where(tx >= n_tx // 2, (n_tx - 1 - tx) * tile_rows + (tile_rows - 2) - row, tx * tile_rows + row)
    col = jnp.where(hi == 1, tile_cols - 2 - col, col)
    key = (col // strips * HALF + row) * strips + col % strips
    key, amount, order = lax.sort((key, amount, lax.iota(jnp.int32, count)), num_keys=1, is_stable=False)
    row = (key // strips) % HALF
    col = key // (strips * HALF) * strips + key % strips
    row, col = (row.astype(jnp.float32), col.astype(jnp.float32))

    own_route = [(b * 2 + t, t * 2 + b) for b in range(2) for t in range(2)]
    other_route = [(b * 2 + t, t * 2 + 1 - b) for b in range(2) for t in range(2)]
    own = lax.ppermute(jnp.stack([row, col, amount]), ("q", "hi"), own_route)
    mine, own = lax.optimization_barrier((jnp.stack([row, col]), own))
    other = lax.ppermute(mine, ("q", "hi"), other_route)
    own = lax.all_gather(own, ("tx", "dom"), axis=0)
    other, own = lax.optimization_barrier((other, own))
    shifts = [(a, c) for a in range(n_tx) for c in range(n_dom)][::-1]
    others = [lax.ppermute(other, ("tx", "dom"), shifted(n_tx, n_dom, shift)) if any(shift) else other for shift in shifts]
    sources_tx = jnp.stack([(tx + a) % n_tx for a, _ in shifts])

    strip_start = (tx * n_dom + dom) * strips
    col_pair = jnp.where(q == 1, jnp.array([[0.375, 0.625]]), jnp.array([[0.625, 0.375]]))

    def settings(list_tx):
        upper = list_tx >= n_tx // 2
        row_pair = jnp.where(upper[:, None], jnp.array([[0.25, 0.75]]), jnp.array([[0.75, 0.25]]))
        pairs = jnp.concatenate([row_pair, jnp.broadcast_to(col_pair, (lists, 2))], 1).astype(jnp.float32)
        return (jnp.concatenate([strip_start[None], upper]).astype(jnp.int32), pairs)

    own_scalars, own_pairs = settings(jnp.arange(lists) // n_dom)
    other_scalars, other_pairs = settings(sources_tx)
    smem, vmem = (pl.BlockSpec(memory_space=pltpu.SMEM), pl.BlockSpec(memory_space=pltpu.VMEM))
    params = pltpu.CompilerParams(vmem_limit_bytes=vmem_limit)

    to_deposit = (own_scalars, *block_ends(own), own_pairs, own)
    charge_shape = (2, pad_cols, HALF + window)
    kick_shape = jax.ShapeDtypeStruct((2, count), jnp.float32)

    angles = np.pi * (np.arange(GRID) + 1) / (2 * (GRID + 1))
    lam = (4.0 * np.sin(angles) ** 2).astype(np.float32)
    lam_e, lam_o = (lam[0::2], lam[1::2])
    lam_k = lax.dynamic_slice_in_dim(jnp.asarray(np.concatenate([lam_e, lam_o])), lax.axis_index(cube) * modes, modes)

    if modes % 128 == 0 and strips % 8 == 0 and piece_rows % strips == 0:
        stored = jnp.asarray(np.stack([part for table in basis_tables() for part in split_table(table)]))
        anywhere = pl.BlockSpec(memory_space=pl.ANY)
        fetched = [pltpu.VMEM(stored.shape, stored.dtype), pltpu.SemaphoreType.DMA((8 * pieces,))]
        outgoing = pltpu.VMEM((devices, pad_cols, modes), jnp.float32)
        by_mode = pl.pallas_call(
            functools.partial(modes_kernel, strips),
            out_shape=jax.ShapeDtypeStruct((devices, pad_cols, modes), jnp.float32),
            in_specs=[smem] * 4 + [vmem, anywhere],
            out_specs=vmem,
            scratch_shapes=[
                pltpu.VMEM(charge_shape, jnp.float32),
                pltpu.VMEM((4, HALF, HALF), jnp.bfloat16),
                fetched[1],
                *deposit_parts(lists, charge_shape),
            ],
            compiler_params=params,
            name="modes",
        )(*to_deposit, stored)
        by_mode, *others = lax.optimization_barrier((by_mode, *others))
        other = jnp.stack(others)
        by_mode = lax.all_to_all(by_mode, cube, 0, 0, tiled=True)
        natural = [(b, a * n_dom + c) for b in range(n_lo) for a in range(n_tx) for c in range(n_dom)]
        straight = [(j // n_dom * n_lo + b) * n_dom + j % n_dom for b, j in natural]
        flipped = [(j // n_dom * n_lo + n_lo - 1 - b) * n_dom + j % n_dom for b, j in natural]
        halves = pl.pallas_call(
            functools.partial(columns_kernel, straight, flipped, lists, strips),
            out_shape=jax.ShapeDtypeStruct((devices, 2, pad_cols, modes), jnp.float32),
            in_specs=[vmem] * 3 + [anywhere],
            out_specs=anywhere,
            scratch_shapes=[*fetched, outgoing, outgoing, pltpu.SemaphoreType.DMA((2,))],
            compiler_params=params,
            name="columns",
        )(by_mode, jnp.asarray(np.stack([lam_e, lam_o])), lam_k[:, None], stored)
        halves = lax.all_to_all(halves, cube, 0, 0, tiled=True)
        to_sample = (other_scalars, *block_ends(other), other_pairs, other)
        fields_shape = jax.ShapeDtypeStruct((2, 2 * pad_cols, HALF + window), jnp.bfloat16)
        early = lists // 2
        *kicks, field_high, field_low = pl.pallas_call(
            functools.partial(kicks_kernel, strips),
            out_shape=[kick_shape] * early + [fields_shape] * 2,
            in_specs=[smem] * 4 + [vmem] * 2 + [anywhere],
            out_specs=[vmem] * (early + 2),
            scratch_shapes=fetched,
            compiler_params=params,
            name="kicks",
        )(*to_sample, halves, stored)
        kicks += pl.pallas_call(
            functools.partial(sample_alone, strips, early),
            out_shape=[kick_shape] * (lists - early),
            in_specs=[smem] * 4 + [vmem] * 3,
            out_specs=[vmem] * (lists - early),
            compiler_params=params,
            name="sample",
        )(*to_sample, field_high, field_low)
    else:
        other = jnp.stack(others)
        to_sample = (other_scalars, *block_ends(other), other_pairs, other)
        tables = [tuple(jnp.asarray(part) for part in split_table(table)) for table in basis_tables()]
        kicks = general(to_deposit, to_sample, tables, lam_e, lam_o, lam_k, (n_tx, n_lo, n_dom), charge_shape, kick_shape)
    kicks = [
        lax.ppermute(kick, ("q", "tx", "hi", "dom"), returned(other_route, n_tx, n_dom, shift))
        for kick, shift in zip(kicks, shifts, strict=True)
    ]
    kicks = functools.reduce(jnp.add, kicks)
    _, kick_x, kick_y = lax.sort((order, kicks[0], kicks[1]), num_keys=1, is_stable=False)
    return momenta + kick_gain * jnp.stack([kick_x, kick_y])[None]


def solution(mesh):
    n_beam, n_tx, n_ty, n_dom = (mesh.shape[name] for name in ("beam", "tx", "ty", "dom"))
    split_mesh = Mesh(mesh.devices.reshape(n_beam, n_tx, 2, n_ty // 2, n_dom), ("q", "tx", "hi", "lo", "dom"))
    where = ("tx", "hi", "lo", "dom")
    placed = (P("q", where), P("q", where), P("q", where), P("q", None, where))
    return jax.shard_map(
        shards,
        mesh=split_mesh,
        in_specs=placed,
        out_specs=P("q", None, where),
        check_vma=False,
    )
```

```python
import functools

import jax
import jax.numpy as jnp
import ml_dtypes
import numpy as np
from jax import lax
from jax.experimental import pallas as pl
from jax.experimental.pallas import tpu as pltpu
from jax.sharding import Mesh
from jax.sharding import PartitionSpec as P

GRID = 2048
HALF = GRID // 2
kick_gain = 2.0
block = 512
window = 256
pieces = 2
piece_rows = HALF // pieces
cube = ("q", "tx", "lo", "dom")
vmem_limit = 48 * 1024 * 1024


def split_table(values):
    high = values.astype(ml_dtypes.bfloat16)
    low = (values - high.astype(np.float64)).astype(ml_dtypes.bfloat16)
    return (high, low)


@functools.lru_cache(maxsize=None)
def basis_tables():
    points = GRID + 1
    position = np.arange(HALF)[:, None] + 1
    wave = np.arange(GRID)[None, :] + 1
    angles = np.pi * ((position * wave) % (2 * points)) / points
    scaling = np.sqrt(2.0 / points)
    sine = scaling * np.sin(angles)
    slope = -scaling * (np.pi * wave / points) * np.cos(angles)
    return (sine[:, 0::2], sine[:, 1::2], slope[:, 0::2], slope[:, 1::2])


def folded_tables():
    points = GRID + 1
    number = np.arange(HALF) + 1
    angles = 2 * np.pi * (number[:, None] * number[None, :] % points) / points
    scaling = np.sqrt(2.0 / points)
    return np.stack([part for table in (np.sin(angles), np.cos(angles)) for part in split_table(scaling * table)])


def alternate(shape, dim):
    return (1 - 2 * (lax.broadcasted_iota(jnp.int32, shape, dim) % 2)).astype(jnp.float32)


def split(values):
    high = lax.reduce_precision(values, 8, 7)
    return (high.astype(jnp.bfloat16), (values - high).astype(jnp.bfloat16))


def dot(left, right, dims):
    return lax.dot_general(left, right, (dims, ((), ())), preferred_element_type=jnp.float32)


def table_left(table, values, contract):
    high, low = split(values)
    width = values.shape[1]
    both = dot(table[0], jnp.concatenate([high, low], 1), ((contract,), (0,)))
    return both[:, :width] + both[:, width:] + dot(table[1], high, ((contract,), (0,)))


def table_right(values, table, contract):
    high, low = split(values)
    rows = values.shape[0]
    both = dot(jnp.concatenate([high, low], 0), table[0], ((1,), (contract,)))
    return both[:rows] + both[rows:] + dot(high, table[1], ((1,), (contract,)))


def pair_weights(index, first, second, rows):
    shape = (rows, index.shape[1])
    at = lax.broadcasted_iota(jnp.int32, shape, 0).astype(jnp.float32).astype(index.dtype)
    one, zero = (jnp.ones((), index.dtype), jnp.zeros((), first.dtype))
    return jnp.where(at == index, first, jnp.where(at == index + one, second, zero))


def short(values):
    return values.astype(jnp.float32).astype(jnp.bfloat16)


def dot_parts(table_high, table_low, values, dims):
    high = values.astype(jnp.bfloat16).astype(jnp.float32)
    rows = values.shape[0]
    both = dot(jnp.concatenate([high, values - high], 0).astype(jnp.bfloat16), table_high, dims)
    return both[:rows] + both[rows:] + dot(high.astype(jnp.bfloat16), table_low, dims)


def windows(strips, start, first, last, which, turn):
    first_row, first_col = (first[which, 0, turn], first[which, 1, turn])
    last_row, last_col = (last[which, 0, turn], last[which, 1, turn])
    least = jnp.where(first_col >= start, first_row, 0) // 128 * 128
    most = jnp.where(last_col < start + strips, last_row, HALF - 2)
    return (least, (most + 1 - least) // window + 1)


def each_window(strips, scalars, first, last, group, item):
    start = scalars[0]

    def bounds(turn, found):
        return tuple(
            (
                low + jnp.where(last[which, 1, turn] < start, 1, 0),
                high + jnp.where(first[which, 1, turn] < start + strips, 1, 0),
            )
            for which, (low, high) in zip(group, found, strict=True)
        )

    found = lax.fori_loop(0, first.shape[2], bounds, tuple((0, 0) for _ in group))
    stride = max(4 // len(group), 1)
    turns = (functools.reduce(jnp.maximum, [high - low for low, high in found]) + stride - 1) // stride
    streams = [
        (place * stride + ahead, which, low + ahead, high)
        for place, (which, (low, high)) in enumerate(zip(group, found, strict=True))
        for ahead in range(stride)
    ]

    def one_turn(step, carry):
        more = []
        for place, which, low, high in streams:
            valid = low + step * stride < high
            turn = jnp.minimum(low + step * stride, first.shape[2] - 1)
            at, count = windows(strips, start, first, last, which, turn)
            item(place, which, turn, pl.multiple_of(at, 128), valid)
            more.append((place, which, turn, at, jnp.where(valid, count, 0)))
        for place, which, turn, at, count in more:

            def one_window(extra, carry, place=place, which=which, turn=turn, at=at):
                item(place, which, turn, pl.multiple_of(at + extra * window, 128), True)
                return carry

            lax.fori_loop(1, count, one_window, 0)
        return carry

    lax.fori_loop(0, turns, one_turn, 0)


def values_of(lists, which, what, turn):
    rows = block // 128
    return jnp.concatenate([lists[which, what, pl.ds(turn * rows + i, 1)] for i in range(rows)], 1)


def cells_of(strips, scalars, lists, which, turn, at, valid):
    row = values_of(lists, which, 0, turn).astype(jnp.int32) - at
    row = jnp.where((row >= -1) & (row < window) & valid, row, -10)
    col = values_of(lists, which, 1, turn).astype(jnp.int32) - scalars[0]
    col = jnp.where((col >= 0) & (col < strips), col, -10)
    return (row, col)


def groups_of(count):
    return [tuple(range(first, min(first + 4, count))) for first in range(0, count, 4)]


def deposit_body(strips, scalars, first, last, weights, lists, charge, parts):
    pad_cols = charge.shape[1]
    tall = -(-pad_cols // 16) * 16
    count = lists.shape[0]
    for part in parts:
        part[...] = jnp.zeros_like(part)

    def half_of(which):
        return which // (count // 2)

    def item(place, which, turn, at, valid):
        row, col = cells_of(strips, scalars, lists, which, turn, at, valid)
        amount = values_of(lists, which, 2, turn)
        near, far = (weights[which, 2] * amount, weights[which, 3] * amount)
        near_high, far_high = (near.astype(jnp.bfloat16), far.astype(jnp.bfloat16))
        near_low = (near - near_high.astype(jnp.float32)).astype(jnp.bfloat16)
        far_low = (far - far_high.astype(jnp.float32)).astype(jnp.bfloat16)
        col = short(col)
        cols = jnp.concatenate(
            [pair_weights(col, near_high, far_high, tall), pair_weights(col, near_low, far_low, tall)], 0
        )
        rows = pair_weights(short(row), short(weights[which, 0]), short(weights[which, 1]), window)
        both = dot(cols, rows, ((1,), (1,)))
        half = half_of(which) if count > 4 else 0
        parts[place][half, :, pl.ds(at, window)] += both[:pad_cols] + both[tall : tall + pad_cols]

    for group in groups_of(count):
        each_window(strips, scalars, first, last, group, item)
    for half in range(2):
        if count > 4:
            used = [part[half] for part in parts]
        else:
            used = [part[0] for which, part in enumerate(parts) if half_of(which) == half]
        charge[half] = functools.reduce(jnp.add, used)


def deposit_parts(count, charge_shape):
    return [pltpu.VMEM((2 if count > 4 else 1, *charge_shape[1:]), jnp.float32)] * min(count, 4)


def sample_body(strips, scalars, first, last, weights, lists, field_high, field_low, kicks, begin):
    pad_cols = field_high.shape[1] // 2
    for kick in kicks:
        kick[...] = jnp.zeros_like(kick)

    def item(place, which, turn, at, valid):
        here = pl.ds(pl.multiple_of(turn * block, block), block)
        half = scalars[1 + which]
        kick = kicks[which - begin]
        row, col = cells_of(strips, scalars, lists, which, turn, at, valid)
        rows = pair_weights(short(row), short(weights[which, 0]), short(weights[which, 1]), window)
        fields = jnp.concatenate([field_high[half, :, pl.ds(at, window)], field_low[half, :, pl.ds(at, window)]], 1)
        near = dot(fields, jnp.concatenate([rows, rows], 0), ((1,), (0,)))
        cols = pair_weights(col.astype(jnp.float32), weights[which, 2], weights[which, 3], pad_cols)
        kick[0:1, here] += jnp.sum(near[:pad_cols] * cols, axis=0, keepdims=True)
        kick[1:2, here] += jnp.sum(near[pad_cols:] * cols, axis=0, keepdims=True)

    for group in groups_of(len(kicks)):
        group = tuple(begin + which for which in group)
        each_window(strips, scalars, first, last, group, item)


def fetch(stored, tables, arrived, parts):
    copies = {part: [] for part in parts}
    for number, (part, piece) in enumerate((part, piece) for part in parts for piece in range(pieces)):
        rows = pl.ds(piece * piece_rows, piece_rows)
        copies[part].append(pltpu.make_async_copy(stored.at[part, rows], tables.at[part, rows], arrived.at[number]))
        copies[part][-1].start()

    def table(part, begin=0, end=pieces):
        for copy in copies[part][begin:end] + copies[part + 1][begin:end]:
            copy.wait()
        rows = slice(begin * piece_rows, end * piece_rows)
        return (tables[part, rows], tables[part + 1, rows])

    return table


def modes_kernel(strips, scalars, first, last, weights, lists, stored, by_mode, charge, tables, arrived, *parts):
    table = fetch(stored, tables, arrived, (0, 1))
    deposit_body(strips, scalars, first, last, weights, lists, charge, parts)
    devices, pad_cols, modes = by_mode.shape
    near, far = (charge[0, :, :HALF], charge[1, :, :HALF])
    high, low = table(0)
    both = jnp.concatenate([(near + far) * alternate((1, HALF), 1), near - far], 0)
    done = dot_parts(high, low, both, ((1,), (0,)))
    for turn in range(devices // 2):
        here = slice(turn * modes, (turn + 1) * modes)
        by_mode[turn] = done[:pad_cols, here]
        by_mode[devices // 2 + turn] = done[pad_cols:, here]


def columns_kernel(order, flipped, per_tile, strips, by_mode, lam, wave, mine, stored, halves, tables, arrived, back_x, back_y, sent):
    table = fetch(stored, tables, arrived, (0, 1, 2, 3))
    sine_parts = table(0)
    modes = by_mode.shape[2]
    near, far = ([], [])
    for place in range(len(order)):
        pair = []
        for here, before in ((order, 0), (flipped, len(order))):
            body = by_mode[before + here[place], :strips]
            if place % per_tile:
                halo = by_mode[before + here[place - 1], strips:]
                body = jnp.concatenate([body[:8] + halo, body[8:]], 0)
            pair.append(body)
        near.append(pair[0] + pair[1])
        far.append(pair[0] - pair[1])
    columns = jnp.concatenate([jnp.concatenate(near, 0).T * alternate((1, HALF), 1), jnp.concatenate(far, 0).T], 0)
    spectrum = dot_parts(*sine_parts, columns, ((1,), (0,)))
    lam_mine, wave_mine = (mine[:, 0:1], mine[:, 1:2])
    hats = ([], [])
    for parity in range(2):
        this = slice(parity, parity + 1)
        hat = spectrum[parity * modes : (parity + 1) * modes] * (1.0 / (lam[this, :] + lam_mine))
        hats[0].append((hat * wave_mine).T)
        hats[1].append((hat * wave[this, :]).T)

    copies = []
    for component, (outgoing, sign) in enumerate(((back_x, 1), (back_y, -1))):
        hat = jnp.concatenate(hats[component], 1)
        hat_high = hat.astype(jnp.bfloat16)
        hat_both = jnp.concatenate([hat_high, (hat - hat_high.astype(jnp.float32)).astype(jnp.bfloat16)], 1)
        parts = sine_parts if component == 0 else table(2)
        for piece in range(pieces):
            high, low = (part[piece * piece_rows : (piece + 1) * piece_rows] for part in parts)
            done = dot(high, hat_both, ((1,), (0,)))
            done = done[:, : 2 * modes] + done[:, 2 * modes :] + dot(low, hat_high, ((1,), (0,)))
            even, odd = (done[:, :modes] * (sign * alternate((piece_rows, modes), 0)), done[:, modes:])
            for before, whose, value in (
                (0, order, even + odd),
                (len(order), flipped, even - odd if sign == 1 else odd - even),
            ):
                for turn in range(piece_rows // strips):
                    place = piece * piece_rows // strips + turn
                    part = value[turn * strips : (turn + 1) * strips]
                    outgoing[before + whose[place], :strips] = part
                    if place % per_tile:
                        outgoing[before + whose[place - 1], strips:] = part[:8]
                    if place % per_tile == per_tile - 1:
                        outgoing[before + whose[place], strips:] = jnp.zeros_like(part[:8])
        copies.append(pltpu.make_async_copy(outgoing, halves.at[:, component], sent.at[component]))
        copies[-1].start()
    for copy in copies:
        copy.wait()


def kicks_kernel(strips, scalars, first, last, weights, lists, halves, stored, *refs):
    kicks, (field_high, field_low, tables, arrived) = (refs[:-4], refs[-4:])
    table = fetch(stored, tables, arrived, (2, 3, 0, 1))
    devices, _, pad_cols, _ = halves.shape
    wide = 2 * pad_cols
    fields = {}
    for component, sign in enumerate((-1, 1)):
        sides = [
            jnp.concatenate([halves[start + turn, component] for turn in range(devices // 2)], 1) for start in (0, devices // 2)
        ]
        both = jnp.concatenate(sides, 0)
        done = 0.0
        for piece in range(pieces):
            rows = slice(piece * piece_rows, (piece + 1) * piece_rows)
            done += dot_parts(*table(2 - 2 * component, piece, piece + 1), both[:, rows], ((1,), (0,)))
        even, odd = (done[:pad_cols] * (sign * alternate((1, HALF), 1)), done[pad_cols:])
        fields[component] = (even + odd, even - odd if sign == 1 else odd - even)
    for half in range(2):
        value = jnp.concatenate([fields[component][half] for component in range(2)], 0)
        high = value.astype(jnp.bfloat16)
        field_high[half, :, :HALF] = high
        field_low[half, :, :HALF] = (value - high.astype(jnp.float32)).astype(jnp.bfloat16)
        beyond = jnp.zeros((wide, window), jnp.bfloat16)
        field_high[half, :, HALF:] = beyond
        field_low[half, :, HALF:] = beyond
    sample_body(strips, scalars, first, last, weights, lists, field_high, field_low, kicks, 0)


def block_ends(lists):
    rows = block // 128
    ends = (lists[:, :2, 0::rows, 0], lists[:, :2, rows - 1 :: rows, 127])
    return tuple(end.astype(jnp.int32) for end in ends)


def deposit_alone(strips, scalars, first, last, weights, lists, charge, *parts):
    deposit_body(strips, scalars, first, last, weights, lists, charge, parts)


def sample_alone(strips, begin, scalars, first, last, weights, lists, field_high, field_low, *kicks):
    sample_body(strips, scalars, first, last, weights, lists, field_high, field_low, kicks, begin)


def shifted(n_tx, n_dom, shift):
    return [
        ((a + shift[0]) % n_tx * n_dom + (c + shift[1]) % n_dom, a * n_dom + c) for a in range(n_tx) for c in range(n_dom)
    ]


def returned(route, n_tx, n_dom, shift):
    pairs = []
    for there, here in route:
        for a in range(n_tx):
            for c in range(n_dom):
                target = ((there // 2 * n_tx + (a + shift[0]) % n_tx) * 2 + there % 2) * n_dom + (c + shift[1]) % n_dom
                pairs.append((((here // 2 * n_tx + a) * 2 + here % 2) * n_dom + c, target))
    return pairs


def general(to_deposit, to_sample, tables, lam_e, lam_o, lam_k, sizes, charge_shape, kick_shape):
    n_tx, n_lo, n_dom = sizes
    devices = 2 * n_tx * n_lo * n_dom
    modes = GRID // devices
    tile_cols = HALF // n_lo
    strips = tile_cols // (n_tx * n_dom)
    pad_cols = charge_shape[1]
    smem, vmem = (pl.BlockSpec(memory_space=pltpu.SMEM), pl.BlockSpec(memory_space=pltpu.VMEM))
    params = pltpu.CompilerParams(vmem_limit_bytes=vmem_limit)
    sine_e, sine_o, slope_e, slope_o = tables
    starts = np.array([b * tile_cols + (a * n_dom + c) * strips for a in range(n_tx) for b in range(n_lo) for c in range(n_dom)])
    offsets = np.arange(pad_cols)
    columns = starts[:, None] + offsets
    kept = (offsets <= strips) & (columns < HALF)
    picked = np.where(kept, columns, 0).reshape(-1)
    used = kept.reshape(-1, 1)
    strip_sine_e, strip_sine_o, strip_slope_e, strip_slope_o = (
        tuple(jnp.asarray(part) for part in split_table(table[picked] * used)) for table in basis_tables()
    )

    charge = pl.pallas_call(
        functools.partial(deposit_alone, strips),
        out_shape=jax.ShapeDtypeStruct(charge_shape, jnp.float32),
        in_specs=[smem] * 4 + [vmem],
        out_specs=vmem,
        scratch_shapes=deposit_parts(n_tx * n_dom, charge_shape),
        compiler_params=params,
        name="deposit",
    )(*to_deposit)[:, :, :HALF]

    even = table_right(charge[0] + charge[1], sine_e, 0)
    odd = table_right(charge[0] - charge[1], sine_o, 0)
    by_mode = jnp.concatenate([even, odd], 1).reshape(pad_cols, devices, modes).transpose(1, 0, 2)
    by_mode = lax.all_to_all(by_mode, cube, 0, 0, tiled=True)

    def flip(part):
        return part.reshape(n_tx, n_lo, n_dom, pad_cols, modes)[:, ::-1].reshape(devices // 2, pad_cols, modes)

    near, far = (by_mode[: devices // 2], flip(by_mode[devices // 2 :]))
    folded = (devices // 2 * pad_cols, modes)
    spectrum_e = table_left(strip_sine_e, (near + far).reshape(folded), 0)
    spectrum_o = table_left(strip_sine_o, (near - far).reshape(folded), 0)
    hat_e = spectrum_e * (1.0 / (lam_e[:, None] + lam_k[None, :]))
    hat_o = spectrum_o * (1.0 / (lam_o[:, None] + lam_k[None, :]))
    shape = (devices // 2, pad_cols, modes)
    along_e = table_left(strip_sine_e, hat_e, 1).reshape(shape)
    along_o = table_left(strip_sine_o, hat_o, 1).reshape(shape)
    across_e = table_left(strip_slope_e, hat_e, 1).reshape(shape)
    across_o = table_left(strip_slope_o, hat_o, 1).reshape(shape)
    halves = jnp.concatenate(
        [
            jnp.stack([along_e + along_o, across_e + across_o], 1),
            jnp.stack([flip(along_e - along_o), flip(across_o - across_e)], 1),
        ],
        0,
    )
    halves = lax.all_to_all(halves, cube, 0, 0, tiled=True)

    halves = halves.transpose(1, 2, 0, 3).reshape(2, pad_cols, GRID)
    x_e = table_right(halves[0, :, :HALF], slope_e, 1)
    x_o = table_right(halves[0, :, HALF:], slope_o, 1)
    y_e = table_right(halves[1, :, :HALF], sine_e, 1)
    y_o = table_right(halves[1, :, HALF:], sine_o, 1)
    field = jnp.stack([jnp.concatenate([x_e + x_o, y_e + y_o], 0), jnp.concatenate([x_o - x_e, y_e - y_o], 0)])
    field = jnp.pad(field, ((0, 0), (0, 0), (0, window)))
    field_high, field_low = split(field)

    return pl.pallas_call(
        functools.partial(sample_alone, strips, 0),
        out_shape=[kick_shape] * (n_tx * n_dom),
        in_specs=[smem] * 4 + [vmem] * 3,
        out_specs=[vmem] * (n_tx * n_dom),
        compiler_params=params,
        name="sample",
    )(*to_sample, field_high, field_low)


def shards(cell_row, cell_col, weights, momenta):
    n_tx, n_lo, n_dom = (lax.axis_size(name) for name in ("tx", "lo", "dom"))
    tile_rows = GRID // n_tx
    tile_cols = HALF // n_lo
    lists = n_tx * n_dom
    strips = tile_cols // lists
    pad_cols = strips + 8
    devices = 2 * n_lo * lists
    modes = GRID // devices
    count = cell_row.shape[1]
    q, hi, lo, tx, dom = (lax.axis_index(name) for name in ("q", "hi", "lo", "tx", "dom"))

    row, col, amount = (cell_row, cell_col, weights[0])
    row = jnp.where(tx >= n_tx // 2, (n_tx - 1 - tx) * tile_rows + (tile_rows - 2) - row, tx * tile_rows + row)
    col = jnp.where(hi == 1, tile_cols - 2 - col, col)
    key = (col // strips * HALF + row) * strips + col % strips
    key, amount, order = lax.sort((key.reshape(-1), amount, lax.iota(jnp.int32, count)), num_keys=1, is_stable=False)
    row = (key // strips) % HALF
    col = key // (strips * HALF) * strips + key % strips
    row, col, amount = (values.astype(jnp.float32).reshape(-1, 128) for values in (row, col, amount))

    own_route = [(b * 2 + t, t * 2 + b) for b in range(2) for t in range(2)]
    other_route = [(b * 2 + t, t * 2 + 1 - b) for b in range(2) for t in range(2)]
    own = lax.ppermute(jnp.stack([row, col, amount]), ("q", "hi"), own_route)
    mine, own = lax.optimization_barrier((jnp.stack([row, col]), own))
    other = lax.ppermute(mine, ("q", "hi"), other_route)
    own = lax.all_gather(own, ("tx", "dom"), axis=0)
    other, own = lax.optimization_barrier((other, own))
    shifts = [(a, c) for a in range(n_tx) for c in range(n_dom)][::-1]
    others = [lax.ppermute(other, ("tx", "dom"), shifted(n_tx, n_dom, shift)) if any(shift) else other for shift in shifts]
    sources_tx = jnp.stack([(tx + a) % n_tx for a, _ in shifts])

    strip_start = (tx * n_dom + dom) * strips
    col_pair = jnp.where(q == 1, jnp.array([[0.375, 0.625]]), jnp.array([[0.625, 0.375]]))

    def settings(list_tx):
        upper = list_tx >= n_tx // 2
        row_pair = jnp.where(upper[:, None], jnp.array([[0.25, 0.75]]), jnp.array([[0.75, 0.25]]))
        pairs = jnp.concatenate([row_pair, jnp.broadcast_to(col_pair, (lists, 2))], 1).astype(jnp.float32)
        return (jnp.concatenate([strip_start[None], upper]).astype(jnp.int32), pairs)

    own_scalars, own_pairs = settings(jnp.arange(lists) // n_dom)
    other_scalars, other_pairs = settings(sources_tx)
    smem, vmem = (pl.BlockSpec(memory_space=pltpu.SMEM), pl.BlockSpec(memory_space=pltpu.VMEM))
    params = pltpu.CompilerParams(vmem_limit_bytes=vmem_limit)

    to_deposit = (own_scalars, *block_ends(own), own_pairs, own)
    charge_shape = (2, pad_cols, HALF + window)
    kick_shape = jax.ShapeDtypeStruct((2, count), jnp.float32)

    angles = np.pi * (np.arange(GRID) + 1) / (2 * (GRID + 1))
    lam = (4.0 * np.sin(angles) ** 2).astype(np.float32)
    lam_e, lam_o = (lam[0::2], lam[1::2])
    lam_k = lax.dynamic_slice_in_dim(jnp.asarray(np.concatenate([lam_e, lam_o])), lax.axis_index(cube) * modes, modes)

    if modes % 128 == 0 and strips % 8 == 0 and piece_rows % strips == 0:
        stored = jnp.asarray(folded_tables())
        anywhere = pl.BlockSpec(memory_space=pl.ANY)
        fetched = [pltpu.VMEM(stored.shape, stored.dtype), pltpu.SemaphoreType.DMA((4 * pieces,))]
        outgoing = pltpu.VMEM((devices, pad_cols, modes), jnp.float32)
        by_mode = pl.pallas_call(
            functools.partial(modes_kernel, strips),
            out_shape=jax.ShapeDtypeStruct((devices, pad_cols, modes), jnp.float32),
            in_specs=[smem] * 4 + [vmem, anywhere],
            out_specs=vmem,
            scratch_shapes=[
                pltpu.VMEM(charge_shape, jnp.float32),
                pltpu.VMEM((2, HALF, HALF), jnp.bfloat16),
                fetched[1],
                *deposit_parts(lists, charge_shape),
            ],
            compiler_params=params,
            name="modes",
        )(*to_deposit, stored)
        by_mode, *others = lax.optimization_barrier((by_mode, *others))
        other = jnp.stack(others)
        by_mode = lax.all_to_all(by_mode, cube, 0, 0, tiled=True)
        order_k = np.concatenate([GRID - 2 - 2 * np.arange(HALF), 2 * np.arange(HALF) + 1])
        wave = (-np.pi * (np.arange(GRID) + 1) / (GRID + 1)).astype(np.float32)
        mine = jnp.asarray(np.stack([lam[order_k], wave[order_k]], 1))
        mine = lax.dynamic_slice_in_dim(mine, lax.axis_index(cube) * modes, modes)
        natural = [(b, a * n_dom + c) for b in range(n_lo) for a in range(n_tx) for c in range(n_dom)]
        straight = [(j // n_dom * n_lo + b) * n_dom + j % n_dom for b, j in natural]
        flipped = [(j // n_dom * n_lo + n_lo - 1 - b) * n_dom + j % n_dom for b, j in natural]
        halves = pl.pallas_call(
            functools.partial(columns_kernel, straight, flipped, lists, strips),
            out_shape=jax.ShapeDtypeStruct((devices, 2, pad_cols, modes), jnp.float32),
            in_specs=[vmem] * 4 + [anywhere],
            out_specs=anywhere,
            scratch_shapes=[*fetched, outgoing, outgoing, pltpu.SemaphoreType.DMA((2,))],
            compiler_params=pltpu.CompilerParams(vmem_limit_bytes=51 * 1024 * 1024),
            name="columns",
        )(by_mode, *(jnp.asarray(values[order_k].reshape(2, HALF)) for values in (lam, wave)), mine, stored)
        halves = lax.all_to_all(halves, cube, 0, 0, tiled=True)
        to_sample = (other_scalars, *block_ends(other), other_pairs, other)
        fields_shape = jax.ShapeDtypeStruct((2, 2 * pad_cols, HALF + window), jnp.bfloat16)
        early = lists // 2
        *kicks, field_high, field_low = pl.pallas_call(
            functools.partial(kicks_kernel, strips),
            out_shape=[kick_shape] * early + [fields_shape] * 2,
            in_specs=[smem] * 4 + [vmem] * 2 + [anywhere],
            out_specs=[vmem] * (early + 2),
            scratch_shapes=fetched,
            compiler_params=params,
            name="kicks",
        )(*to_sample, halves, stored)
        kicks += pl.pallas_call(
            functools.partial(sample_alone, strips, early),
            out_shape=[kick_shape] * (lists - early),
            in_specs=[smem] * 4 + [vmem] * 3,
            out_specs=[vmem] * (lists - early),
            compiler_params=params,
            name="sample",
        )(*to_sample, field_high, field_low)
    else:
        other = jnp.stack(others)
        to_sample = (other_scalars, *block_ends(other), other_pairs, other)
        tables = [tuple(jnp.asarray(part) for part in split_table(table)) for table in basis_tables()]
        kicks = general(to_deposit, to_sample, tables, lam_e, lam_o, lam_k, (n_tx, n_lo, n_dom), charge_shape, kick_shape)
    kicks = [
        lax.ppermute(kick, ("q", "tx", "hi", "dom"), returned(other_route, n_tx, n_dom, shift))
        for kick, shift in zip(kicks, shifts, strict=True)
    ]
    kicks = functools.reduce(jnp.add, kicks)
    _, kick_x, kick_y = lax.sort((order, kicks[0], kicks[1]), num_keys=1, is_stable=False)
    return momenta + kick_gain * jnp.stack([kick_x, kick_y])[None]


def solution(mesh):
    n_beam, n_tx, n_ty, n_dom = (mesh.shape[name] for name in ("beam", "tx", "ty", "dom"))
    split_mesh = Mesh(mesh.devices.reshape(n_beam, n_tx, 2, n_ty // 2, n_dom), ("q", "tx", "hi", "lo", "dom"))
    where = ("tx", "hi", "lo", "dom")
    placed = (P("q", where), P("q", where), P("q", where), P("q", None, where))
    return jax.shard_map(
        shards,
        mesh=split_mesh,
        in_specs=placed,
        out_specs=P("q", None, where),
        check_vma=False,
    )
```

```python
import functools

import jax
import jax.numpy as jnp
import ml_dtypes
import numpy as np
from jax import lax
from jax.experimental import pallas as pl
from jax.experimental.pallas import tpu as pltpu
from jax.sharding import Mesh
from jax.sharding import PartitionSpec as P

GRID = 2048
HALF = GRID // 2
kick_gain = 2.0
block = 512
window = 256
pieces = 2
piece_rows = HALF // pieces
cube = ("q", "tx", "lo", "dom")
vmem_limit = 48 * 1024 * 1024


def split_table(values):
    high = values.astype(ml_dtypes.bfloat16)
    low = (values - high.astype(np.float64)).astype(ml_dtypes.bfloat16)
    return (high, low)


@functools.lru_cache(maxsize=None)
def basis_tables():
    points = GRID + 1
    position = np.arange(HALF)[:, None] + 1
    wave = np.arange(GRID)[None, :] + 1
    angles = np.pi * ((position * wave) % (2 * points)) / points
    scaling = np.sqrt(2.0 / points)
    sine = scaling * np.sin(angles)
    slope = -scaling * (np.pi * wave / points) * np.cos(angles)
    return (sine[:, 0::2], sine[:, 1::2], slope[:, 0::2], slope[:, 1::2])


def folded_tables():
    points = GRID + 1
    number = np.arange(HALF) + 1
    angles = 2 * np.pi * (number[:, None] * number[None, :] % points) / points
    scaling = np.sqrt(2.0 / points)
    return np.stack([part for table in (np.sin(angles), np.cos(angles)) for part in split_table(scaling * table)])


def alternate(shape, dim):
    return (1 - 2 * (lax.broadcasted_iota(jnp.int32, shape, dim) % 2)).astype(jnp.float32)


def split(values):
    high = lax.reduce_precision(values, 8, 7)
    return (high.astype(jnp.bfloat16), (values - high).astype(jnp.bfloat16))


def dot(left, right, dims):
    return lax.dot_general(left, right, (dims, ((), ())), preferred_element_type=jnp.float32)


def table_left(table, values, contract):
    high, low = split(values)
    width = values.shape[1]
    both = dot(table[0], jnp.concatenate([high, low], 1), ((contract,), (0,)))
    return both[:, :width] + both[:, width:] + dot(table[1], high, ((contract,), (0,)))


def table_right(values, table, contract):
    high, low = split(values)
    rows = values.shape[0]
    both = dot(jnp.concatenate([high, low], 0), table[0], ((1,), (contract,)))
    return both[:rows] + both[rows:] + dot(high, table[1], ((1,), (contract,)))


def pair_weights(index, first, second, rows):
    shape = (rows, index.shape[1])
    at = lax.broadcasted_iota(jnp.int32, shape, 0).astype(jnp.float32).astype(index.dtype)
    one, zero = (jnp.ones((), index.dtype), jnp.zeros((), first.dtype))
    return jnp.where(at == index, first, jnp.where(at == index + one, second, zero))


def short(values):
    return values.astype(jnp.float32).astype(jnp.bfloat16)


def dot_parts(table_high, table_low, values, dims):
    high = values.astype(jnp.bfloat16).astype(jnp.float32)
    rows = values.shape[0]
    both = dot(jnp.concatenate([high, values - high], 0).astype(jnp.bfloat16), table_high, dims)
    return both[:rows] + both[rows:] + dot(high.astype(jnp.bfloat16), table_low, dims)


def windows(strips, start, first, last, which, turn):
    first_row, first_col = (first[which, 0, turn], first[which, 1, turn])
    last_row, last_col = (last[which, 0, turn], last[which, 1, turn])
    least = jnp.where(first_col >= start, first_row, 0) // 128 * 128
    most = jnp.where(last_col < start + strips, last_row, HALF - 2)
    return (least, (most + 1 - least) // window + 1)


def strip_blocks(strips, scalars, first, last, group):
    start = scalars[0]

    def bounds(turn, found):
        return tuple(
            (
                low + jnp.where(last[which, 1, turn] < start, 1, 0),
                high + jnp.where(first[which, 1, turn] < start + strips, 1, 0),
            )
            for which, (low, high) in zip(group, found, strict=True)
        )

    return lax.fori_loop(0, first.shape[2], bounds, tuple((0, 0) for _ in group), unroll=8)


def each_window(strips, scalars, first, last, group, found, item):
    start = scalars[0]
    stride = max(4 // len(group), 1)
    turns = (functools.reduce(jnp.maximum, [high - low for low, high in found]) + stride - 1) // stride
    streams = [
        (place * stride + ahead, which, low + ahead, high)
        for place, (which, (low, high)) in enumerate(zip(group, found, strict=True))
        for ahead in range(stride)
    ]

    def one_turn(step, carry):
        more = []
        for place, which, low, high in streams:
            valid = low + step * stride < high
            turn = jnp.minimum(low + step * stride, first.shape[2] - 1)
            at, count = windows(strips, start, first, last, which, turn)
            item(place, which, turn, pl.multiple_of(at, 128), valid)
            more.append((place, which, turn, at, jnp.where(valid, count, 0)))
        for place, which, turn, at, count in more:

            def one_window(extra, carry, place=place, which=which, turn=turn, at=at):
                item(place, which, turn, pl.multiple_of(at + extra * window, 128), True)
                return carry

            lax.fori_loop(1, count, one_window, 0)
        return carry

    lax.fori_loop(0, turns, one_turn, 0)


def values_of(lists, which, what, turn):
    rows = block // 128
    return jnp.concatenate([lists[which, what, pl.ds(turn * rows + i, 1)] for i in range(rows)], 1)


def cells_of(strips, scalars, lists, which, turn, at, valid):
    row = values_of(lists, which, 0, turn).astype(jnp.int32) - at
    row = jnp.where((row >= -1) & (row < window) & valid, row, -10)
    col = values_of(lists, which, 1, turn).astype(jnp.int32) - scalars[0]
    col = jnp.where((col >= 0) & (col < strips), col, -10)
    return (row, col)


def groups_of(count):
    return [tuple(range(first, min(first + 4, count))) for first in range(0, count, 4)]


def deposit_body(strips, scalars, first, last, weights, lists, charge, parts):
    pad_cols = charge.shape[1]
    tall = -(-pad_cols // 16) * 16
    count = lists.shape[0]
    for part in parts:
        part[...] = jnp.zeros_like(part)

    def half_of(which):
        return which // (count // 2)

    def item(place, which, turn, at, valid):
        row, col = cells_of(strips, scalars, lists, which, turn, at, valid)
        amount = values_of(lists, which, 2, turn)
        near, far = (weights[which, 2] * amount, weights[which, 3] * amount)
        near_high, far_high = (near.astype(jnp.bfloat16), far.astype(jnp.bfloat16))
        near_low = (near - near_high.astype(jnp.float32)).astype(jnp.bfloat16)
        far_low = (far - far_high.astype(jnp.float32)).astype(jnp.bfloat16)
        col = short(col)
        cols = jnp.concatenate(
            [pair_weights(col, near_high, far_high, tall), pair_weights(col, near_low, far_low, tall)], 0
        )
        rows = pair_weights(short(row), short(weights[which, 0]), short(weights[which, 1]), window)
        both = dot(cols, rows, ((1,), (1,)))
        half = half_of(which) if count > 4 else 0
        parts[place][half, :, pl.ds(at, window)] += both[:pad_cols] + both[tall : tall + pad_cols]

    for group in groups_of(count):
        each_window(strips, scalars, first, last, group, strip_blocks(strips, scalars, first, last, group), item)
    for half in range(2):
        if count > 4:
            used = [part[half] for part in parts]
        else:
            used = [part[0] for which, part in enumerate(parts) if half_of(which) == half]
        charge[half] = functools.reduce(jnp.add, used)


def deposit_parts(count, charge_shape):
    return [pltpu.VMEM((2 if count > 4 else 1, *charge_shape[1:]), jnp.float32)] * min(count, 4)


def sample_start(strips, scalars, first, last, kicks, begin):
    for kick in kicks:
        kick[...] = jnp.zeros_like(kick)
    groups = [tuple(begin + which for which in group) for group in groups_of(len(kicks))]
    return [(group, strip_blocks(strips, scalars, first, last, group)) for group in groups]


def sample_body(strips, scalars, first, last, weights, lists, field_high, field_low, kicks, begin, started):
    pad_cols = field_high.shape[1] // 2

    def item(place, which, turn, at, valid):
        half = scalars[1 + which]
        kick = kicks[which - begin]
        row, col = cells_of(strips, scalars, lists, which, turn, at, valid)
        rows = pair_weights(short(row), short(weights[which, 0]), short(weights[which, 1]), window)
        fields = jnp.concatenate([field_high[half, :, pl.ds(at, window)], field_low[half, :, pl.ds(at, window)]], 1)
        near = dot(fields, jnp.concatenate([rows, rows], 0), ((1,), (0,)))
        cols = pair_weights(col.astype(jnp.float32), weights[which, 2], weights[which, 3], pad_cols)
        for component, part in enumerate((near[:pad_cols], near[pad_cols:])):
            total = jnp.sum(part * cols, axis=0, keepdims=True)
            for i in range(block // 128):
                kick[component, pl.ds(turn * (block // 128) + i, 1)] += total[:, i * 128 : (i + 1) * 128]

    for group, found in started:
        each_window(strips, scalars, first, last, group, found, item)


def fetch(stored, tables, arrived, parts):
    copies = {part: [] for part in parts}
    for number, (part, piece) in enumerate((part, piece) for part in parts for piece in range(pieces)):
        rows = pl.ds(piece * piece_rows, piece_rows)
        copies[part].append(pltpu.make_async_copy(stored.at[part, rows], tables.at[part, rows], arrived.at[number]))
        copies[part][-1].start()

    def table(part, begin=0, end=pieces):
        for copy in copies[part][begin:end] + copies[part + 1][begin:end]:
            copy.wait()
        rows = slice(begin * piece_rows, end * piece_rows)
        return (tables[part, rows], tables[part + 1, rows])

    return table


def modes_kernel(strips, scalars, first, last, weights, lists, stored, sent_modes, charge, tables, arrived, by_mode, sent, *parts):
    table = fetch(stored, tables, arrived, (0, 1))
    deposit_body(strips, scalars, first, last, weights, lists, charge, parts)
    devices, pad_cols, modes = by_mode.shape
    near, far = (charge[0, :, :HALF], charge[1, :, :HALF])
    high, low = table(0)
    both = jnp.concatenate([(near + far) * alternate((1, HALF), 1), near - far], 0)
    copies = []
    quarter = devices // 4
    for part in range(2):
        done = dot_parts(high[:, part * HALF // 2 : (part + 1) * HALF // 2], low[:, part * HALF // 2 : (part + 1) * HALF // 2], both, ((1,), (0,)))
        for turn in range(quarter):
            here = slice(turn * modes, (turn + 1) * modes)
            by_mode[part * quarter + turn] = done[:pad_cols, here]
            by_mode[devices // 2 + part * quarter + turn] = done[pad_cols:, here]
        for parity in range(2):
            here = pl.ds(parity * (devices // 2) + part * quarter, quarter)
            copies.append(pltpu.make_async_copy(by_mode.at[here], sent_modes.at[here], sent.at[2 * part + parity]))
            copies[-1].start()
    for copy in copies:
        copy.wait()


def columns_kernel(order, flipped, per_tile, strips, by_mode, lam, wave, mine, stored, halves, tables, arrived, outgoing, sent):
    table = fetch(stored, tables, arrived, (0, 1, 2, 3))
    sine_parts = table(0)
    modes = by_mode.shape[2]
    near, far = ([], [])
    for place in range(len(order)):
        pair = []
        for here, before in ((order, 0), (flipped, len(order))):
            body = by_mode[before + here[place], :strips]
            if place % per_tile:
                halo = by_mode[before + here[place - 1], strips:]
                body = jnp.concatenate([body[:8] + halo, body[8:]], 0)
            pair.append(body)
        near.append(pair[0] + pair[1])
        far.append(pair[0] - pair[1])
    columns = jnp.concatenate([jnp.concatenate(near, 0).T * alternate((1, HALF), 1), jnp.concatenate(far, 0).T], 0)
    spectrum = dot_parts(*sine_parts, columns, ((1,), (0,)))
    lam_mine, wave_mine = (mine[:, 0:1], mine[:, 1:2])
    hats = ([], [])
    for parity in range(2):
        this = slice(parity, parity + 1)
        hat = spectrum[parity * modes : (parity + 1) * modes] * (1.0 / (lam[this, :] + lam_mine))
        hats[0].append((hat * wave_mine).T)
        hats[1].append((hat * wave[this, :]).T)

    copies = []
    wide = 2 * strips
    outgoing[:, wide:] = jnp.zeros((outgoing.shape[0], 8, modes), jnp.float32)
    for component, sign in enumerate((1, -1)):
        hat = jnp.concatenate(hats[component], 1)
        hat_high = hat.astype(jnp.bfloat16)
        hat_both = jnp.concatenate([hat_high, (hat - hat_high.astype(jnp.float32)).astype(jnp.bfloat16)], 1)
        parts = sine_parts if component == 0 else table(2)
        for piece in range(pieces):
            high, low = (part[piece * piece_rows : (piece + 1) * piece_rows] for part in parts)
            done = dot(high, hat_both, ((1,), (0,)))
            done = done[:, : 2 * modes] + done[:, 2 * modes :] + dot(low, hat_high, ((1,), (0,)))
            even, odd = (done[:, :modes] * (sign * alternate((piece_rows, modes), 0)), done[:, modes:])
            for before, whose, value in (
                (0, order, even + odd),
                (len(order), flipped, even - odd if sign == 1 else odd - even),
            ):
                for turn in range(piece_rows // strips):
                    place = piece * piece_rows // strips + turn
                    part = value[turn * strips : (turn + 1) * strips]
                    outgoing[before + whose[place], component * strips : (component + 1) * strips] = part
                    if place % per_tile:
                        outgoing[before + whose[place - 1], wide + component : wide + component + 1] = part[:1]
        here = pl.ds(0, strips) if component == 0 else pl.ds(strips, strips + 8)
        copies.append(pltpu.make_async_copy(outgoing.at[:, here], halves.at[:, here], sent.at[component]))
        copies[-1].start()
    for copy in copies:
        copy.wait()


def kicks_kernel(strips, scalars, first, last, weights, lists, halves, stored, *refs):
    kicks, (field_high, field_low, tables, arrived) = (refs[:-4], refs[-4:])
    table = fetch(stored, tables, arrived, (2, 3, 0, 1))
    started = sample_start(strips, scalars, first, last, kicks, 0)
    devices = halves.shape[0]
    pad_cols = strips + 8
    wide = 2 * pad_cols
    fields = {}
    for component, sign in enumerate((-1, 1)):
        sides = []
        for start in (0, devices // 2):
            for here in (slice(component * strips, (component + 1) * strips), slice(2 * strips, 2 * strips + 8)):
                sides.append(jnp.concatenate([halves[start + turn, here] for turn in range(devices // 2)], 1))
            after = jnp.broadcast_to(sides[-1][component : component + 1], sides[-1].shape)
            sides[-1] = jnp.where(lax.broadcasted_iota(jnp.int32, after.shape, 0) == 0, after, 0.0)
        both = jnp.concatenate(sides, 0)
        done = 0.0
        for piece in range(pieces):
            rows = slice(piece * piece_rows, (piece + 1) * piece_rows)
            done += dot_parts(*table(2 - 2 * component, piece, piece + 1), both[:, rows], ((1,), (0,)))
        even, odd = (done[:pad_cols] * (sign * alternate((1, HALF), 1)), done[pad_cols:])
        fields[component] = (even + odd, even - odd if sign == 1 else odd - even)
    for half in range(2):
        value = jnp.concatenate([fields[component][half] for component in range(2)], 0)
        high = value.astype(jnp.bfloat16)
        field_high[half, :, :HALF] = high
        field_low[half, :, :HALF] = (value - high.astype(jnp.float32)).astype(jnp.bfloat16)
        beyond = jnp.zeros((wide, window), jnp.bfloat16)
        field_high[half, :, HALF:] = beyond
        field_low[half, :, HALF:] = beyond
    sample_body(strips, scalars, first, last, weights, lists, field_high, field_low, kicks, 0, started)


def block_ends(lists):
    rows = block // 128
    ends = (lists[:, :2, 0::rows, 0], lists[:, :2, rows - 1 :: rows, 127])
    return tuple(end.astype(jnp.int32) for end in ends)


def deposit_alone(strips, scalars, first, last, weights, lists, charge, *parts):
    deposit_body(strips, scalars, first, last, weights, lists, charge, parts)


def sample_alone(strips, begin, scalars, first, last, weights, lists, field_high, field_low, *kicks):
    started = sample_start(strips, scalars, first, last, kicks, begin)
    sample_body(strips, scalars, first, last, weights, lists, field_high, field_low, kicks, begin, started)


def shifted(n_tx, n_dom, shift):
    return [
        ((a + shift[0]) % n_tx * n_dom + (c + shift[1]) % n_dom, a * n_dom + c) for a in range(n_tx) for c in range(n_dom)
    ]


def returned(route, n_tx, n_dom, shift):
    pairs = []
    for there, here in route:
        for a in range(n_tx):
            for c in range(n_dom):
                target = ((there // 2 * n_tx + (a + shift[0]) % n_tx) * 2 + there % 2) * n_dom + (c + shift[1]) % n_dom
                pairs.append((((here // 2 * n_tx + a) * 2 + here % 2) * n_dom + c, target))
    return pairs


def general(to_deposit, to_sample, tables, lam_e, lam_o, lam_k, sizes, charge_shape, kick_shape):
    n_tx, n_lo, n_dom = sizes
    devices = 2 * n_tx * n_lo * n_dom
    modes = GRID // devices
    tile_cols = HALF // n_lo
    strips = tile_cols // (n_tx * n_dom)
    pad_cols = charge_shape[1]
    smem, vmem = (pl.BlockSpec(memory_space=pltpu.SMEM), pl.BlockSpec(memory_space=pltpu.VMEM))
    params = pltpu.CompilerParams(vmem_limit_bytes=vmem_limit)
    sine_e, sine_o, slope_e, slope_o = tables
    starts = np.array([b * tile_cols + (a * n_dom + c) * strips for a in range(n_tx) for b in range(n_lo) for c in range(n_dom)])
    offsets = np.arange(pad_cols)
    columns = starts[:, None] + offsets
    kept = (offsets <= strips) & (columns < HALF)
    picked = np.where(kept, columns, 0).reshape(-1)
    used = kept.reshape(-1, 1)
    strip_sine_e, strip_sine_o, strip_slope_e, strip_slope_o = (
        tuple(jnp.asarray(part) for part in split_table(table[picked] * used)) for table in basis_tables()
    )

    charge = pl.pallas_call(
        functools.partial(deposit_alone, strips),
        out_shape=jax.ShapeDtypeStruct(charge_shape, jnp.float32),
        in_specs=[smem] * 4 + [vmem],
        out_specs=vmem,
        scratch_shapes=deposit_parts(n_tx * n_dom, charge_shape),
        compiler_params=params,
        name="deposit",
    )(*to_deposit)[:, :, :HALF]

    even = table_right(charge[0] + charge[1], sine_e, 0)
    odd = table_right(charge[0] - charge[1], sine_o, 0)
    by_mode = jnp.concatenate([even, odd], 1).reshape(pad_cols, devices, modes).transpose(1, 0, 2)
    by_mode = lax.all_to_all(by_mode, cube, 0, 0, tiled=True)

    def flip(part):
        return part.reshape(n_tx, n_lo, n_dom, pad_cols, modes)[:, ::-1].reshape(devices // 2, pad_cols, modes)

    near, far = (by_mode[: devices // 2], flip(by_mode[devices // 2 :]))
    folded = (devices // 2 * pad_cols, modes)
    spectrum_e = table_left(strip_sine_e, (near + far).reshape(folded), 0)
    spectrum_o = table_left(strip_sine_o, (near - far).reshape(folded), 0)
    hat_e = spectrum_e * (1.0 / (lam_e[:, None] + lam_k[None, :]))
    hat_o = spectrum_o * (1.0 / (lam_o[:, None] + lam_k[None, :]))
    shape = (devices // 2, pad_cols, modes)
    along_e = table_left(strip_sine_e, hat_e, 1).reshape(shape)
    along_o = table_left(strip_sine_o, hat_o, 1).reshape(shape)
    across_e = table_left(strip_slope_e, hat_e, 1).reshape(shape)
    across_o = table_left(strip_slope_o, hat_o, 1).reshape(shape)
    halves = jnp.concatenate(
        [
            jnp.stack([along_e + along_o, across_e + across_o], 1),
            jnp.stack([flip(along_e - along_o), flip(across_o - across_e)], 1),
        ],
        0,
    )
    halves = lax.all_to_all(halves, cube, 0, 0, tiled=True)

    halves = halves.transpose(1, 2, 0, 3).reshape(2, pad_cols, GRID)
    x_e = table_right(halves[0, :, :HALF], slope_e, 1)
    x_o = table_right(halves[0, :, HALF:], slope_o, 1)
    y_e = table_right(halves[1, :, :HALF], sine_e, 1)
    y_o = table_right(halves[1, :, HALF:], sine_o, 1)
    field = jnp.stack([jnp.concatenate([x_e + x_o, y_e + y_o], 0), jnp.concatenate([x_o - x_e, y_e - y_o], 0)])
    field = jnp.pad(field, ((0, 0), (0, 0), (0, window)))
    field_high, field_low = split(field)

    return pl.pallas_call(
        functools.partial(sample_alone, strips, 0),
        out_shape=[kick_shape] * (n_tx * n_dom),
        in_specs=[smem] * 4 + [vmem] * 3,
        out_specs=[vmem] * (n_tx * n_dom),
        compiler_params=params,
        name="sample",
    )(*to_sample, field_high, field_low)


def shards(cell_row, cell_col, weights, momenta):
    n_tx, n_lo, n_dom = (lax.axis_size(name) for name in ("tx", "lo", "dom"))
    tile_rows = GRID // n_tx
    tile_cols = HALF // n_lo
    lists = n_tx * n_dom
    strips = tile_cols // lists
    pad_cols = strips + 8
    devices = 2 * n_lo * lists
    modes = GRID // devices
    count = cell_row.shape[1]
    q, hi, lo, tx, dom = (lax.axis_index(name) for name in ("q", "hi", "lo", "tx", "dom"))

    row, col, amount = (cell_row, cell_col, weights[0])
    row = jnp.where(tx >= n_tx // 2, (n_tx - 1 - tx) * tile_rows + (tile_rows - 2) - row, tx * tile_rows + row)
    col = jnp.where(hi == 1, tile_cols - 2 - col, col)
    key = (col // strips * HALF + row) * strips + col % strips
    key, amount, order = lax.sort((key.reshape(-1), amount, lax.iota(jnp.int32, count)), num_keys=1, is_stable=False)
    row = (key // strips) % HALF
    col = key // (strips * HALF) * strips + key % strips
    row, col, amount = (values.astype(jnp.float32).reshape(-1, 128) for values in (row, col, amount))

    own_route = [(b * 2 + t, t * 2 + b) for b in range(2) for t in range(2)]
    other_route = [(b * 2 + t, t * 2 + 1 - b) for b in range(2) for t in range(2)]
    own = lax.ppermute(jnp.stack([row, col, amount]), ("q", "hi"), own_route)
    mine, own = lax.optimization_barrier((jnp.stack([row, col]), own))
    other = lax.ppermute(mine, ("q", "hi"), other_route)
    own = lax.all_gather(own, ("tx", "dom"), axis=0)
    other, own = lax.optimization_barrier((other, own))
    shifts = [(a, c) for a in range(n_tx) for c in range(n_dom)][::-1]
    others = [lax.ppermute(other, ("tx", "dom"), shifted(n_tx, n_dom, shift)) if any(shift) else other for shift in shifts]
    sources_tx = jnp.stack([(tx + a) % n_tx for a, _ in shifts])

    strip_start = (tx * n_dom + dom) * strips
    col_pair = jnp.where(q == 1, jnp.array([[0.375, 0.625]]), jnp.array([[0.625, 0.375]]))

    def settings(list_tx):
        upper = list_tx >= n_tx // 2
        row_pair = jnp.where(upper[:, None], jnp.array([[0.25, 0.75]]), jnp.array([[0.75, 0.25]]))
        pairs = jnp.concatenate([row_pair, jnp.broadcast_to(col_pair, (lists, 2))], 1).astype(jnp.float32)
        return (jnp.concatenate([strip_start[None], upper]).astype(jnp.int32), pairs)

    own_scalars, own_pairs = settings(jnp.arange(lists) // n_dom)
    other_scalars, other_pairs = settings(sources_tx)
    smem, vmem = (pl.BlockSpec(memory_space=pltpu.SMEM), pl.BlockSpec(memory_space=pltpu.VMEM))
    params = pltpu.CompilerParams(vmem_limit_bytes=vmem_limit)

    to_deposit = (own_scalars, *block_ends(own), own_pairs, own)
    charge_shape = (2, pad_cols, HALF + window)
    kick_shape = jax.ShapeDtypeStruct((2, count // 128, 128), jnp.float32)

    angles = np.pi * (np.arange(GRID) + 1) / (2 * (GRID + 1))
    lam = (4.0 * np.sin(angles) ** 2).astype(np.float32)
    lam_e, lam_o = (lam[0::2], lam[1::2])
    lam_k = lax.dynamic_slice_in_dim(jnp.asarray(np.concatenate([lam_e, lam_o])), lax.axis_index(cube) * modes, modes)

    if modes % 128 == 0 and strips % 8 == 0 and piece_rows % strips == 0:
        stored = jnp.asarray(folded_tables())
        anywhere = pl.BlockSpec(memory_space=pl.ANY)
        fetched = [pltpu.VMEM(stored.shape, stored.dtype), pltpu.SemaphoreType.DMA((4 * pieces,))]
        outgoing = pltpu.VMEM((devices, 2 * strips + 8, modes), jnp.float32)
        by_mode = pl.pallas_call(
            functools.partial(modes_kernel, strips),
            out_shape=jax.ShapeDtypeStruct((devices, pad_cols, modes), jnp.float32),
            in_specs=[smem] * 4 + [vmem, anywhere],
            out_specs=anywhere,
            scratch_shapes=[
                pltpu.VMEM(charge_shape, jnp.float32),
                pltpu.VMEM((2, HALF, HALF), jnp.bfloat16),
                fetched[1],
                pltpu.VMEM((devices, pad_cols, modes), jnp.float32),
                pltpu.SemaphoreType.DMA((4,)),
                *deposit_parts(lists, charge_shape),
            ],
            compiler_params=params,
            name="modes",
        )(*to_deposit, stored)
        by_mode, *others = lax.optimization_barrier((by_mode, *others))
        other = jnp.stack(others)
        by_mode = lax.all_to_all(by_mode, cube, 0, 0, tiled=True)
        order_k = np.concatenate([GRID - 2 - 2 * np.arange(HALF), 2 * np.arange(HALF) + 1])
        wave = (-np.pi * (np.arange(GRID) + 1) / (GRID + 1)).astype(np.float32)
        mine = jnp.asarray(np.stack([lam[order_k], wave[order_k]], 1))
        mine = lax.dynamic_slice_in_dim(mine, lax.axis_index(cube) * modes, modes)
        natural = [(b, a * n_dom + c) for b in range(n_lo) for a in range(n_tx) for c in range(n_dom)]
        straight = [(j // n_dom * n_lo + b) * n_dom + j % n_dom for b, j in natural]
        flipped = [(j // n_dom * n_lo + n_lo - 1 - b) * n_dom + j % n_dom for b, j in natural]
        halves = pl.pallas_call(
            functools.partial(columns_kernel, straight, flipped, lists, strips),
            out_shape=jax.ShapeDtypeStruct(outgoing.shape, jnp.float32),
            in_specs=[vmem] * 4 + [anywhere],
            out_specs=anywhere,
            scratch_shapes=[*fetched, outgoing, pltpu.SemaphoreType.DMA((2,))],
            compiler_params=pltpu.CompilerParams(vmem_limit_bytes=51 * 1024 * 1024),
            name="columns",
        )(by_mode, *(jnp.asarray(values[order_k].reshape(2, HALF)) for values in (lam, wave)), mine, stored)
        halves = lax.all_to_all(halves, cube, 0, 0, tiled=True)
        to_sample = (other_scalars, *block_ends(other), other_pairs, other)
        fields_shape = jax.ShapeDtypeStruct((2, 2 * pad_cols, HALF + window), jnp.bfloat16)
        early = lists // 2
        *kicks, field_high, field_low = pl.pallas_call(
            functools.partial(kicks_kernel, strips),
            out_shape=[kick_shape] * early + [fields_shape] * 2,
            in_specs=[smem] * 4 + [vmem] * 2 + [anywhere],
            out_specs=[vmem] * (early + 2),
            scratch_shapes=fetched,
            compiler_params=params,
            name="kicks",
        )(*to_sample, halves, stored)
        kicks += pl.pallas_call(
            functools.partial(sample_alone, strips, early),
            out_shape=[kick_shape] * (lists - early),
            in_specs=[smem] * 4 + [vmem] * 3,
            out_specs=[vmem] * (lists - early),
            compiler_params=params,
            name="sample",
        )(*to_sample, field_high, field_low)
    else:
        other = jnp.stack(others)
        to_sample = (other_scalars, *block_ends(other), other_pairs, other)
        tables = [tuple(jnp.asarray(part) for part in split_table(table)) for table in basis_tables()]
        kicks = general(to_deposit, to_sample, tables, lam_e, lam_o, lam_k, (n_tx, n_lo, n_dom), charge_shape, kick_shape)
    kicks = [
        lax.ppermute(kick, ("q", "tx", "hi", "dom"), returned(other_route, n_tx, n_dom, shift))
        for kick, shift in zip(kicks, shifts, strict=True)
    ]
    kicks = functools.reduce(jnp.add, kicks)
    _, kick_x, kick_y = lax.sort((order, kicks[0].reshape(-1), kicks[1].reshape(-1)), num_keys=1, is_stable=False)
    return momenta + kick_gain * jnp.stack([kick_x, kick_y])[None]


def solution(mesh):
    n_beam, n_tx, n_ty, n_dom = (mesh.shape[name] for name in ("beam", "tx", "ty", "dom"))
    split_mesh = Mesh(mesh.devices.reshape(n_beam, n_tx, 2, n_ty // 2, n_dom), ("q", "tx", "hi", "lo", "dom"))
    where = ("tx", "hi", "lo", "dom")
    placed = (P("q", where), P("q", where), P("q", where), P("q", None, where))
    return jax.shard_map(
        shards,
        mesh=split_mesh,
        in_specs=placed,
        out_specs=P("q", None, where),
        check_vma=False,
    )
```

```python
import functools

import jax
import jax.numpy as jnp
import ml_dtypes
import numpy as np
from jax import lax
from jax.experimental import pallas as pl
from jax.experimental.pallas import tpu as pltpu
from jax.sharding import Mesh
from jax.sharding import PartitionSpec as P

GRID = 2048
HALF = GRID // 2
kick_gain = 2.0
block = 512
window = 256
pieces = 2
piece_rows = HALF // pieces
cube = ("q", "tx", "lo", "dom")
vmem_limit = 48 * 1024 * 1024


def split_table(values):
    high = values.astype(ml_dtypes.bfloat16)
    low = (values - high.astype(np.float64)).astype(ml_dtypes.bfloat16)
    return (high, low)


@functools.lru_cache(maxsize=None)
def basis_tables():
    points = GRID + 1
    position = np.arange(HALF)[:, None] + 1
    wave = np.arange(GRID)[None, :] + 1
    angles = np.pi * ((position * wave) % (2 * points)) / points
    scaling = np.sqrt(2.0 / points)
    sine = scaling * np.sin(angles)
    slope = -scaling * (np.pi * wave / points) * np.cos(angles)
    return (sine[:, 0::2], sine[:, 1::2], slope[:, 0::2], slope[:, 1::2])


def folded_tables():
    points = GRID + 1
    number = np.arange(HALF) + 1
    angles = 2 * np.pi * (number[:, None] * number[None, :] % points) / points
    scaling = np.sqrt(2.0 / points)
    return np.stack([part for table in (np.sin(angles), np.cos(angles)) for part in split_table(scaling * table)])


def alternate(shape, dim):
    return (1 - 2 * (lax.broadcasted_iota(jnp.int32, shape, dim) % 2)).astype(jnp.float32)


def split(values):
    high = lax.reduce_precision(values, 8, 7)
    return (high.astype(jnp.bfloat16), (values - high).astype(jnp.bfloat16))


def dot(left, right, dims):
    return lax.dot_general(left, right, (dims, ((), ())), preferred_element_type=jnp.float32)


def table_left(table, values, contract):
    high, low = split(values)
    width = values.shape[1]
    both = dot(table[0], jnp.concatenate([high, low], 1), ((contract,), (0,)))
    return both[:, :width] + both[:, width:] + dot(table[1], high, ((contract,), (0,)))


def table_right(values, table, contract):
    high, low = split(values)
    rows = values.shape[0]
    both = dot(jnp.concatenate([high, low], 0), table[0], ((1,), (contract,)))
    return both[:rows] + both[rows:] + dot(high, table[1], ((1,), (contract,)))


def pair_weights(index, first, second, rows):
    shape = (rows, index.shape[1])
    at = lax.broadcasted_iota(jnp.int32, shape, 0).astype(jnp.float32).astype(index.dtype)
    one, zero = (jnp.ones((), index.dtype), jnp.zeros((), first.dtype))
    return jnp.where(at == index, first, jnp.where(at == index + one, second, zero))


def short(values):
    return values.astype(jnp.float32).astype(jnp.bfloat16)


def dot_parts(table_high, table_low, values, dims):
    high = values.astype(jnp.bfloat16).astype(jnp.float32)
    rows = values.shape[0]
    both = dot(jnp.concatenate([high, values - high], 0).astype(jnp.bfloat16), table_high, dims)
    return both[:rows] + both[rows:] + dot(high.astype(jnp.bfloat16), table_low, dims)


def windows(strips, start, first, last, which, turn):
    first_row, first_col = (first[which, 0, turn], first[which, 1, turn])
    last_row, last_col = (last[which, 0, turn], last[which, 1, turn])
    least = jnp.where(first_col >= start, first_row, 0) // 128 * 128
    most = jnp.where(last_col < start + strips, last_row, HALF - 2)
    return (least, (most + 1 - least) // window + 1)


def strip_blocks(strips, scalars, first, last, group):
    start = scalars[0]

    def bounds(turn, found):
        return tuple(
            (
                low + jnp.where(last[which, 1, turn] < start, 1, 0),
                high + jnp.where(first[which, 1, turn] < start + strips, 1, 0),
            )
            for which, (low, high) in zip(group, found, strict=True)
        )

    return lax.fori_loop(0, first.shape[2], bounds, tuple((0, 0) for _ in group), unroll=8)


def each_window(strips, scalars, first, last, group, found, item):
    start = scalars[0]
    stride = max(4 // len(group), 1)
    turns = (functools.reduce(jnp.maximum, [high - low for low, high in found]) + stride - 1) // stride
    streams = [
        (place * stride + ahead, which, low + ahead, high)
        for place, (which, (low, high)) in enumerate(zip(group, found, strict=True))
        for ahead in range(stride)
    ]

    def one_turn(step, carry):
        more = []
        for place, which, low, high in streams:
            valid = low + step * stride < high
            turn = jnp.minimum(low + step * stride, first.shape[2] - 1)
            at, count = windows(strips, start, first, last, which, turn)
            item(place, which, turn, pl.multiple_of(at, 128), valid)
            more.append((place, which, turn, at, jnp.where(valid, count, 0)))
        for place, which, turn, at, count in more:

            def one_window(extra, carry, place=place, which=which, turn=turn, at=at):
                item(place, which, turn, pl.multiple_of(at + extra * window, 128), True)
                return carry

            lax.fori_loop(1, count, one_window, 0)
        return carry

    lax.fori_loop(0, turns, one_turn, 0)


def values_of(lists, which, what, turn):
    rows = block // 128
    return jnp.concatenate([lists[which, what, pl.ds(turn * rows + i, 1)] for i in range(rows)], 1)


def cells_of(strips, scalars, lists, which, turn, at, valid):
    row = values_of(lists, which, 0, turn).astype(jnp.int32) - at
    row = jnp.where((row >= -1) & (row < window) & valid, row, -10)
    col = values_of(lists, which, 1, turn).astype(jnp.int32) - scalars[0]
    col = jnp.where((col >= 0) & (col < strips), col, -10)
    return (row, col)


def groups_of(count):
    return [tuple(range(first, min(first + 4, count))) for first in range(0, count, 4)]


def deposit_body(strips, scalars, first, last, weights, lists, charge, parts):
    pad_cols = charge.shape[1]
    tall = -(-pad_cols // 16) * 16
    count = lists.shape[0]
    for part in parts:
        part[...] = jnp.zeros_like(part)

    def half_of(which):
        return which // (count // 2)

    def item(place, which, turn, at, valid):
        row, col = cells_of(strips, scalars, lists, which, turn, at, valid)
        amount = values_of(lists, which, 2, turn)
        near, far = (weights[which, 2] * amount, weights[which, 3] * amount)
        near_high, far_high = (near.astype(jnp.bfloat16), far.astype(jnp.bfloat16))
        near_low = (near - near_high.astype(jnp.float32)).astype(jnp.bfloat16)
        far_low = (far - far_high.astype(jnp.float32)).astype(jnp.bfloat16)
        col = short(col)
        cols = jnp.concatenate(
            [pair_weights(col, near_high, far_high, tall), pair_weights(col, near_low, far_low, tall)], 0
        )
        rows = pair_weights(short(row), short(weights[which, 0]), short(weights[which, 1]), window)
        both = dot(cols, rows, ((1,), (1,)))
        half = half_of(which) if count > 4 else 0
        parts[place][half, :, pl.ds(at, window)] += both[:pad_cols] + both[tall : tall + pad_cols]

    for group in groups_of(count):
        each_window(strips, scalars, first, last, group, strip_blocks(strips, scalars, first, last, group), item)
    for half in range(2):
        if count > 4:
            used = [part[half] for part in parts]
        else:
            used = [part[0] for which, part in enumerate(parts) if half_of(which) == half]
        charge[half] = functools.reduce(jnp.add, used)


def deposit_parts(count, charge_shape):
    return [pltpu.VMEM((2 if count > 4 else 1, *charge_shape[1:]), jnp.float32)] * min(count, 4)


def sample_start(strips, scalars, first, last, kicks, begin):
    for kick in kicks:
        kick[...] = jnp.zeros_like(kick)
    groups = [tuple(begin + which for which in group) for group in groups_of(len(kicks))]
    return [(group, strip_blocks(strips, scalars, first, last, group)) for group in groups]


def sample_body(strips, scalars, first, last, weights, lists, field_high, field_low, kicks, begin, started):
    pad_cols = field_high.shape[1] // 2

    def item(place, which, turn, at, valid):
        half = scalars[1 + which]
        kick = kicks[which - begin]
        row, col = cells_of(strips, scalars, lists, which, turn, at, valid)
        rows = pair_weights(short(row), short(weights[which, 0]), short(weights[which, 1]), window)
        fields = jnp.concatenate([field_high[half, :, pl.ds(at, window)], field_low[half, :, pl.ds(at, window)]], 1)
        near = dot(fields, jnp.concatenate([rows, rows], 0), ((1,), (0,)))
        cols = pair_weights(col.astype(jnp.float32), weights[which, 2], weights[which, 3], pad_cols)
        for component, part in enumerate((near[:pad_cols], near[pad_cols:])):
            total = jnp.sum(part * cols, axis=0, keepdims=True)
            for i in range(block // 128):
                kick[component, pl.ds(turn * (block // 128) + i, 1)] += total[:, i * 128 : (i + 1) * 128]

    for group, found in started:
        each_window(strips, scalars, first, last, group, found, item)


def fetch(stored, tables, arrived, parts):
    copies = {part: [] for part in parts}
    for number, (part, piece) in enumerate((part, piece) for part in parts for piece in range(pieces)):
        rows = pl.ds(piece * piece_rows, piece_rows)
        copies[part].append(pltpu.make_async_copy(stored.at[part, rows], tables.at[part, rows], arrived.at[number]))
        copies[part][-1].start()

    def table(part, begin=0, end=pieces):
        for copy in copies[part][begin:end] + copies[part + 1][begin:end]:
            copy.wait()
        rows = slice(begin * piece_rows, end * piece_rows)
        return (tables[part, rows], tables[part + 1, rows])

    return table


def modes_kernel(strips, scalars, first, last, weights, lists, stored, sent_modes, charge, tables, arrived, by_mode, sent, *parts):
    table = fetch(stored, tables, arrived, (0, 1))
    deposit_body(strips, scalars, first, last, weights, lists, charge, parts)
    devices, pad_cols, modes = by_mode.shape
    near, far = (charge[0, :, :HALF], charge[1, :, :HALF])
    high, low = table(0)
    both = jnp.concatenate([(near + far) * alternate((1, HALF), 1), near - far], 0)
    copies = []
    quarter = devices // 4
    for part in range(2):
        done = dot_parts(high[:, part * HALF // 2 : (part + 1) * HALF // 2], low[:, part * HALF // 2 : (part + 1) * HALF // 2], both, ((1,), (0,)))
        for turn in range(quarter):
            here = slice(turn * modes, (turn + 1) * modes)
            by_mode[part * quarter + turn] = done[:pad_cols, here]
            by_mode[devices // 2 + part * quarter + turn] = done[pad_cols:, here]
        for parity in range(2):
            here = pl.ds(parity * (devices // 2) + part * quarter, quarter)
            copies.append(pltpu.make_async_copy(by_mode.at[here], sent_modes.at[here], sent.at[2 * part + parity]))
            copies[-1].start()
    for copy in copies:
        copy.wait()


def columns_kernel(order, flipped, per_tile, strips, by_mode, lam, wave, mine, stored, halves, tables, arrived, outgoing, sent):
    table = fetch(stored, tables, arrived, (0, 1, 2, 3))
    sine_parts = table(0)
    modes = by_mode.shape[2]
    near, far = ([], [])
    for place in range(len(order)):
        pair = []
        for here, before in ((order, 0), (flipped, len(order))):
            body = by_mode[before + here[place], :strips]
            if place % per_tile:
                halo = by_mode[before + here[place - 1], strips:]
                body = jnp.concatenate([body[:8] + halo, body[8:]], 0)
            pair.append(body)
        near.append(pair[0] + pair[1])
        far.append(pair[0] - pair[1])
    columns = jnp.concatenate([jnp.concatenate(near, 0).T * alternate((1, HALF), 1), jnp.concatenate(far, 0).T], 0)
    spectrum = dot_parts(*sine_parts, columns, ((1,), (0,)))
    lam_mine, wave_mine = (mine[:, 0:1], mine[:, 1:2])
    hats = ([], [])
    for parity in range(2):
        this = slice(parity, parity + 1)
        hat = spectrum[parity * modes : (parity + 1) * modes] * (1.0 / (lam[this, :] + lam_mine))
        hats[0].append((hat * wave_mine).T)
        hats[1].append((hat * wave[this, :]).T)

    copies = []
    wide = 2 * strips
    outgoing[:, wide:] = jnp.zeros((outgoing.shape[0], 8, modes), jnp.float32)
    for component, sign in enumerate((1, -1)):
        hat = jnp.concatenate(hats[component], 1)
        hat_high = hat.astype(jnp.bfloat16)
        hat_both = jnp.concatenate([hat_high, (hat - hat_high.astype(jnp.float32)).astype(jnp.bfloat16)], 1)
        parts = sine_parts if component == 0 else table(2)
        for piece in range(pieces):
            high, low = (part[piece * piece_rows : (piece + 1) * piece_rows] for part in parts)
            done = dot(high, hat_both, ((1,), (0,)))
            done = done[:, : 2 * modes] + done[:, 2 * modes :] + dot(low, hat_high, ((1,), (0,)))
            even, odd = (done[:, :modes] * (sign * alternate((piece_rows, modes), 0)), done[:, modes:])
            for before, whose, value in (
                (0, order, even + odd),
                (len(order), flipped, even - odd if sign == 1 else odd - even),
            ):
                for turn in range(piece_rows // strips):
                    place = piece * piece_rows // strips + turn
                    part = value[turn * strips : (turn + 1) * strips]
                    outgoing[before + whose[place], component * strips : (component + 1) * strips] = part
                    if place % per_tile:
                        outgoing[before + whose[place - 1], wide + component : wide + component + 1] = part[:1]
        here = pl.ds(0, strips) if component == 0 else pl.ds(strips, strips + 8)
        copies.append(pltpu.make_async_copy(outgoing.at[:, here], halves.at[:, here], sent.at[component]))
        copies[-1].start()
    for copy in copies:
        copy.wait()


def kicks_kernel(strips, scalars, first, last, weights, lists, halves, stored, *refs):
    kicks, (field_high, field_low, tables, arrived) = (refs[:-4], refs[-4:])
    table = fetch(stored, tables, arrived, (2, 3, 0, 1))
    started = sample_start(strips, scalars, first, last, kicks, 0)
    devices = halves.shape[0]
    pad_cols = strips + 8
    wide = 2 * pad_cols
    fields = {}
    for component, sign in enumerate((-1, 1)):
        sides = []
        for start in (0, devices // 2):
            for here in (slice(component * strips, (component + 1) * strips), slice(2 * strips, 2 * strips + 8)):
                sides.append(jnp.concatenate([halves[start + turn, here] for turn in range(devices // 2)], 1))
            after = jnp.broadcast_to(sides[-1][component : component + 1], sides[-1].shape)
            sides[-1] = jnp.where(lax.broadcasted_iota(jnp.int32, after.shape, 0) == 0, after, 0.0)
        both = jnp.concatenate(sides, 0)
        done = 0.0
        for piece in range(pieces):
            rows = slice(piece * piece_rows, (piece + 1) * piece_rows)
            done += dot_parts(*table(2 - 2 * component, piece, piece + 1), both[:, rows], ((1,), (0,)))
        even, odd = (done[:pad_cols] * (sign * alternate((1, HALF), 1)), done[pad_cols:])
        fields[component] = (even + odd, even - odd if sign == 1 else odd - even)
    for half in range(2):
        value = jnp.concatenate([fields[component][half] for component in range(2)], 0)
        high = value.astype(jnp.bfloat16)
        field_high[half, :, :HALF] = high
        field_low[half, :, :HALF] = (value - high.astype(jnp.float32)).astype(jnp.bfloat16)
        beyond = jnp.zeros((wide, window), jnp.bfloat16)
        field_high[half, :, HALF:] = beyond
        field_low[half, :, HALF:] = beyond
    sample_body(strips, scalars, first, last, weights, lists, field_high, field_low, kicks, 0, started)


def block_ends(lists):
    rows = block // 128
    ends = (lists[:, :2, 0::rows, 0], lists[:, :2, rows - 1 :: rows, 127])
    return tuple(end.astype(jnp.int32) for end in ends)


def deposit_alone(strips, scalars, first, last, weights, lists, charge, *parts):
    deposit_body(strips, scalars, first, last, weights, lists, charge, parts)


def sample_alone(strips, begin, scalars, first, last, weights, lists, field_high, field_low, *kicks):
    started = sample_start(strips, scalars, first, last, kicks, begin)
    sample_body(strips, scalars, first, last, weights, lists, field_high, field_low, kicks, begin, started)


def shifted(n_tx, n_dom, shift):
    return [
        ((a + shift[0]) % n_tx * n_dom + (c + shift[1]) % n_dom, a * n_dom + c) for a in range(n_tx) for c in range(n_dom)
    ]


def returned(route, n_tx, n_dom, shift):
    pairs = []
    for there, here in route:
        for a in range(n_tx):
            for c in range(n_dom):
                target = ((there // 2 * n_tx + (a + shift[0]) % n_tx) * 2 + there % 2) * n_dom + (c + shift[1]) % n_dom
                pairs.append((((here // 2 * n_tx + a) * 2 + here % 2) * n_dom + c, target))
    return pairs


def general(to_deposit, to_sample, tables, lam_e, lam_o, lam_k, sizes, charge_shape, kick_shape):
    n_tx, n_lo, n_dom = sizes
    devices = 2 * n_tx * n_lo * n_dom
    modes = GRID // devices
    tile_cols = HALF // n_lo
    strips = tile_cols // (n_tx * n_dom)
    pad_cols = charge_shape[1]
    smem, vmem = (pl.BlockSpec(memory_space=pltpu.SMEM), pl.BlockSpec(memory_space=pltpu.VMEM))
    params = pltpu.CompilerParams(vmem_limit_bytes=vmem_limit)
    sine_e, sine_o, slope_e, slope_o = tables
    starts = np.array([b * tile_cols + (a * n_dom + c) * strips for a in range(n_tx) for b in range(n_lo) for c in range(n_dom)])
    offsets = np.arange(pad_cols)
    columns = starts[:, None] + offsets
    kept = (offsets <= strips) & (columns < HALF)
    picked = np.where(kept, columns, 0).reshape(-1)
    used = kept.reshape(-1, 1)
    strip_sine_e, strip_sine_o, strip_slope_e, strip_slope_o = (
        tuple(jnp.asarray(part) for part in split_table(table[picked] * used)) for table in basis_tables()
    )

    charge = pl.pallas_call(
        functools.partial(deposit_alone, strips),
        out_shape=jax.ShapeDtypeStruct(charge_shape, jnp.float32),
        in_specs=[smem] * 4 + [vmem],
        out_specs=vmem,
        scratch_shapes=deposit_parts(n_tx * n_dom, charge_shape),
        compiler_params=params,
        name="deposit",
    )(*to_deposit)[:, :, :HALF]

    even = table_right(charge[0] + charge[1], sine_e, 0)
    odd = table_right(charge[0] - charge[1], sine_o, 0)
    by_mode = jnp.concatenate([even, odd], 1).reshape(pad_cols, devices, modes).transpose(1, 0, 2)
    by_mode = lax.all_to_all(by_mode, cube, 0, 0, tiled=True)

    def flip(part):
        return part.reshape(n_tx, n_lo, n_dom, pad_cols, modes)[:, ::-1].reshape(devices // 2, pad_cols, modes)

    near, far = (by_mode[: devices // 2], flip(by_mode[devices // 2 :]))
    folded = (devices // 2 * pad_cols, modes)
    spectrum_e = table_left(strip_sine_e, (near + far).reshape(folded), 0)
    spectrum_o = table_left(strip_sine_o, (near - far).reshape(folded), 0)
    hat_e = spectrum_e * (1.0 / (lam_e[:, None] + lam_k[None, :]))
    hat_o = spectrum_o * (1.0 / (lam_o[:, None] + lam_k[None, :]))
    shape = (devices // 2, pad_cols, modes)
    along_e = table_left(strip_sine_e, hat_e, 1).reshape(shape)
    along_o = table_left(strip_sine_o, hat_o, 1).reshape(shape)
    across_e = table_left(strip_slope_e, hat_e, 1).reshape(shape)
    across_o = table_left(strip_slope_o, hat_o, 1).reshape(shape)
    halves = jnp.concatenate(
        [
            jnp.stack([along_e + along_o, across_e + across_o], 1),
            jnp.stack([flip(along_e - along_o), flip(across_o - across_e)], 1),
        ],
        0,
    )
    halves = lax.all_to_all(halves, cube, 0, 0, tiled=True)

    halves = halves.transpose(1, 2, 0, 3).reshape(2, pad_cols, GRID)
    x_e = table_right(halves[0, :, :HALF], slope_e, 1)
    x_o = table_right(halves[0, :, HALF:], slope_o, 1)
    y_e = table_right(halves[1, :, :HALF], sine_e, 1)
    y_o = table_right(halves[1, :, HALF:], sine_o, 1)
    field = jnp.stack([jnp.concatenate([x_e + x_o, y_e + y_o], 0), jnp.concatenate([x_o - x_e, y_e - y_o], 0)])
    field = jnp.pad(field, ((0, 0), (0, 0), (0, window)))
    field_high, field_low = split(field)

    return pl.pallas_call(
        functools.partial(sample_alone, strips, 0),
        out_shape=[kick_shape] * (n_tx * n_dom),
        in_specs=[smem] * 4 + [vmem] * 3,
        out_specs=[vmem] * (n_tx * n_dom),
        compiler_params=params,
        name="sample",
    )(*to_sample, field_high, field_low)


def shards(cell_row, cell_col, weights, momenta):
    n_tx, n_lo, n_dom = (lax.axis_size(name) for name in ("tx", "lo", "dom"))
    tile_rows = GRID // n_tx
    tile_cols = HALF // n_lo
    lists = n_tx * n_dom
    strips = tile_cols // lists
    pad_cols = strips + 8
    devices = 2 * n_lo * lists
    modes = GRID // devices
    count = cell_row.shape[1]
    q, hi, lo, tx, dom = (lax.axis_index(name) for name in ("q", "hi", "lo", "tx", "dom"))

    row, col = lax.optimization_barrier((cell_row.reshape(-1, 128), cell_col.reshape(-1, 128)))
    amount = weights[0]
    row = jnp.where(tx >= n_tx // 2, (n_tx - 1 - tx) * tile_rows + (tile_rows - 2) - row, tx * tile_rows + row)
    col = jnp.where(hi == 1, tile_cols - 2 - col, col)
    strip_bits = strips.bit_length() - 1
    key = ((lax.shift_right_logical(col, strip_bits) * HALF + row) << strip_bits) + (col & (strips - 1))
    key, amount, order = lax.sort((key.reshape(-1), amount, lax.iota(jnp.int32, count)), num_keys=1, is_stable=False)
    row = lax.shift_right_logical(key, strip_bits) & (HALF - 1)
    col = (key // (strips * HALF) << strip_bits) + (key & (strips - 1))
    row, col, amount = (values.astype(jnp.float32).reshape(-1, 128) for values in (row, col, amount))

    own_route = [(b * 2 + t, t * 2 + b) for b in range(2) for t in range(2)]
    other_route = [(b * 2 + t, t * 2 + 1 - b) for b in range(2) for t in range(2)]
    own = lax.ppermute(jnp.stack([row, col, amount]), ("q", "hi"), own_route)
    mine, own = lax.optimization_barrier((jnp.stack([row, col]), own))
    other = lax.ppermute(mine, ("q", "hi"), other_route)
    own = lax.all_gather(own, ("tx", "dom"), axis=0)
    other, own = lax.optimization_barrier((other, own))
    shifts = [(a, c) for a in range(n_tx) for c in range(n_dom)][::-1]
    others = [lax.ppermute(other, ("tx", "dom"), shifted(n_tx, n_dom, shift)) if any(shift) else other for shift in shifts]
    sources_tx = jnp.stack([(tx + a) % n_tx for a, _ in shifts])

    strip_start = (tx * n_dom + dom) * strips
    col_pair = jnp.where(q == 1, jnp.array([[0.375, 0.625]]), jnp.array([[0.625, 0.375]]))

    def settings(list_tx):
        upper = list_tx >= n_tx // 2
        row_pair = jnp.where(upper[:, None], jnp.array([[0.25, 0.75]]), jnp.array([[0.75, 0.25]]))
        pairs = jnp.concatenate([row_pair, jnp.broadcast_to(col_pair, (lists, 2))], 1).astype(jnp.float32)
        return (jnp.concatenate([strip_start[None], upper]).astype(jnp.int32), pairs)

    own_scalars, own_pairs = settings(jnp.arange(lists) // n_dom)
    other_scalars, other_pairs = settings(sources_tx)
    smem, vmem = (pl.BlockSpec(memory_space=pltpu.SMEM), pl.BlockSpec(memory_space=pltpu.VMEM))
    params = pltpu.CompilerParams(vmem_limit_bytes=vmem_limit)

    to_deposit = (own_scalars, *block_ends(own), own_pairs, own)
    charge_shape = (2, pad_cols, HALF + window)
    kick_shape = jax.ShapeDtypeStruct((2, count // 128, 128), jnp.float32)

    angles = np.pi * (np.arange(GRID) + 1) / (2 * (GRID + 1))
    lam = (4.0 * np.sin(angles) ** 2).astype(np.float32)
    lam_e, lam_o = (lam[0::2], lam[1::2])
    lam_k = lax.dynamic_slice_in_dim(jnp.asarray(np.concatenate([lam_e, lam_o])), lax.axis_index(cube) * modes, modes)

    if modes % 128 == 0 and strips % 8 == 0 and piece_rows % strips == 0:
        stored = jnp.asarray(folded_tables())
        anywhere = pl.BlockSpec(memory_space=pl.ANY)
        fetched = [pltpu.VMEM(stored.shape, stored.dtype), pltpu.SemaphoreType.DMA((4 * pieces,))]
        outgoing = pltpu.VMEM((devices, 2 * strips + 8, modes), jnp.float32)
        by_mode = pl.pallas_call(
            functools.partial(modes_kernel, strips),
            out_shape=jax.ShapeDtypeStruct((devices, pad_cols, modes), jnp.float32),
            in_specs=[smem] * 4 + [vmem, anywhere],
            out_specs=anywhere,
            scratch_shapes=[
                pltpu.VMEM(charge_shape, jnp.float32),
                pltpu.VMEM((2, HALF, HALF), jnp.bfloat16),
                fetched[1],
                pltpu.VMEM((devices, pad_cols, modes), jnp.float32),
                pltpu.SemaphoreType.DMA((4,)),
                *deposit_parts(lists, charge_shape),
            ],
            compiler_params=params,
            name="modes",
        )(*to_deposit, stored)
        by_mode, *others = lax.optimization_barrier((by_mode, *others))
        other = jnp.stack(others)
        by_mode = lax.all_to_all(by_mode, cube, 0, 0, tiled=True)
        order_k = np.concatenate([GRID - 2 - 2 * np.arange(HALF), 2 * np.arange(HALF) + 1])
        wave = (-np.pi * (np.arange(GRID) + 1) / (GRID + 1)).astype(np.float32)
        mine = jnp.asarray(np.stack([lam[order_k], wave[order_k]], 1))
        mine = lax.dynamic_slice_in_dim(mine, lax.axis_index(cube) * modes, modes)
        natural = [(b, a * n_dom + c) for b in range(n_lo) for a in range(n_tx) for c in range(n_dom)]
        straight = [(j // n_dom * n_lo + b) * n_dom + j % n_dom for b, j in natural]
        flipped = [(j // n_dom * n_lo + n_lo - 1 - b) * n_dom + j % n_dom for b, j in natural]
        halves = pl.pallas_call(
            functools.partial(columns_kernel, straight, flipped, lists, strips),
            out_shape=jax.ShapeDtypeStruct(outgoing.shape, jnp.float32),
            in_specs=[vmem] * 4 + [anywhere],
            out_specs=anywhere,
            scratch_shapes=[*fetched, outgoing, pltpu.SemaphoreType.DMA((2,))],
            compiler_params=pltpu.CompilerParams(vmem_limit_bytes=51 * 1024 * 1024),
            name="columns",
        )(by_mode, *(jnp.asarray(values[order_k].reshape(2, HALF)) for values in (lam, wave)), mine, stored)
        halves = lax.all_to_all(halves, cube, 0, 0, tiled=True)
        to_sample = (other_scalars, *block_ends(other), other_pairs, other)
        fields_shape = jax.ShapeDtypeStruct((2, 2 * pad_cols, HALF + window), jnp.bfloat16)
        early = lists // 2
        *kicks, field_high, field_low = pl.pallas_call(
            functools.partial(kicks_kernel, strips),
            out_shape=[kick_shape] * early + [fields_shape] * 2,
            in_specs=[smem] * 4 + [vmem] * 2 + [anywhere],
            out_specs=[vmem] * (early + 2),
            scratch_shapes=fetched,
            compiler_params=params,
            name="kicks",
        )(*to_sample, halves, stored)
        kicks += pl.pallas_call(
            functools.partial(sample_alone, strips, early),
            out_shape=[kick_shape] * (lists - early),
            in_specs=[smem] * 4 + [vmem] * 3,
            out_specs=[vmem] * (lists - early),
            compiler_params=params,
            name="sample",
        )(*to_sample, field_high, field_low)
    else:
        other = jnp.stack(others)
        to_sample = (other_scalars, *block_ends(other), other_pairs, other)
        tables = [tuple(jnp.asarray(part) for part in split_table(table)) for table in basis_tables()]
        kicks = general(to_deposit, to_sample, tables, lam_e, lam_o, lam_k, (n_tx, n_lo, n_dom), charge_shape, kick_shape)
    kicks = [
        lax.ppermute(kick, ("q", "tx", "hi", "dom"), returned(other_route, n_tx, n_dom, shift))
        for kick, shift in zip(kicks, shifts, strict=True)
    ]
    kicks = functools.reduce(jnp.add, kicks)
    _, kick_x, kick_y = lax.sort((order, kicks[0].reshape(-1), kicks[1].reshape(-1)), num_keys=1, is_stable=False)
    return momenta + kick_gain * jnp.stack([kick_x, kick_y])[None]


def solution(mesh):
    n_beam, n_tx, n_ty, n_dom = (mesh.shape[name] for name in ("beam", "tx", "ty", "dom"))
    split_mesh = Mesh(mesh.devices.reshape(n_beam, n_tx, 2, n_ty // 2, n_dom), ("q", "tx", "hi", "lo", "dom"))
    where = ("tx", "hi", "lo", "dom")
    placed = (P("q", where), P("q", where), P("q", where), P("q", None, where))
    return jax.shard_map(
        shards,
        mesh=split_mesh,
        in_specs=placed,
        out_specs=P("q", None, where),
        check_vma=False,
    )
```

```python
import functools

import jax
import jax.numpy as jnp
import ml_dtypes
import numpy as np
from jax import lax
from jax.experimental import pallas as pl
from jax.experimental.pallas import tpu as pltpu
from jax.sharding import Mesh
from jax.sharding import PartitionSpec as P

GRID = 2048
HALF = GRID // 2
kick_gain = 2.0
block = 512
window = 256
pieces = 2
piece_rows = HALF // pieces
cube = ("q", "tx", "lo", "dom")
vmem_limit = 48 * 1024 * 1024


def split_table(values):
    high = values.astype(ml_dtypes.bfloat16)
    low = (values - high.astype(np.float64)).astype(ml_dtypes.bfloat16)
    return (high, low)


@functools.lru_cache(maxsize=None)
def basis_tables():
    points = GRID + 1
    position = np.arange(HALF)[:, None] + 1
    wave = np.arange(GRID)[None, :] + 1
    angles = np.pi * ((position * wave) % (2 * points)) / points
    scaling = np.sqrt(2.0 / points)
    sine = scaling * np.sin(angles)
    slope = -scaling * (np.pi * wave / points) * np.cos(angles)
    return (sine[:, 0::2], sine[:, 1::2], slope[:, 0::2], slope[:, 1::2])


def folded_tables():
    points = GRID + 1
    number = np.arange(HALF) + 1
    angles = 2 * np.pi * (number[:, None] * number[None, :] % points) / points
    scaling = np.sqrt(2.0 / points)
    return np.stack([part for table in (np.sin(angles), np.cos(angles)) for part in split_table(scaling * table)])


def alternate(shape, dim):
    return (1 - 2 * (lax.broadcasted_iota(jnp.int32, shape, dim) % 2)).astype(jnp.float32)


def split(values):
    high = lax.reduce_precision(values, 8, 7)
    return (high.astype(jnp.bfloat16), (values - high).astype(jnp.bfloat16))


def dot(left, right, dims):
    return lax.dot_general(left, right, (dims, ((), ())), preferred_element_type=jnp.float32)


def table_left(table, values, contract):
    high, low = split(values)
    width = values.shape[1]
    both = dot(table[0], jnp.concatenate([high, low], 1), ((contract,), (0,)))
    return both[:, :width] + both[:, width:] + dot(table[1], high, ((contract,), (0,)))


def table_right(values, table, contract):
    high, low = split(values)
    rows = values.shape[0]
    both = dot(jnp.concatenate([high, low], 0), table[0], ((1,), (contract,)))
    return both[:rows] + both[rows:] + dot(high, table[1], ((1,), (contract,)))


def pair_weights(index, first, second, rows):
    shape = (rows, index.shape[1])
    at = lax.broadcasted_iota(jnp.int32, shape, 0).astype(jnp.float32).astype(index.dtype)
    one, zero = (jnp.ones((), index.dtype), jnp.zeros((), first.dtype))
    return jnp.where(at == index, first, jnp.where(at == index + one, second, zero))


def short(values):
    return values.astype(jnp.float32).astype(jnp.bfloat16)


def dot_parts(table_high, table_low, values, dims):
    high = values.astype(jnp.bfloat16).astype(jnp.float32)
    rows = values.shape[0]
    both = dot(jnp.concatenate([high, values - high], 0).astype(jnp.bfloat16), table_high, dims)
    return both[:rows] + both[rows:] + dot(high.astype(jnp.bfloat16), table_low, dims)


def windows(strips, start, first, last, which, turn):
    first_row, first_col = (first[which, 0, turn], first[which, 1, turn])
    last_row, last_col = (last[which, 0, turn], last[which, 1, turn])
    least = jnp.where(first_col >= start, first_row, 0) // 128 * 128
    most = jnp.where(last_col < start + strips, last_row, HALF - 2)
    return (least, (most + 1 - least) // window + 1)


def strip_blocks(strips, scalars, first, last, group):
    start = scalars[0]

    def bounds(turn, found):
        return tuple(
            (
                low + jnp.where(last[which, 1, turn] < start, 1, 0),
                high + jnp.where(first[which, 1, turn] < start + strips, 1, 0),
            )
            for which, (low, high) in zip(group, found, strict=True)
        )

    return lax.fori_loop(0, first.shape[2], bounds, tuple((0, 0) for _ in group), unroll=8)


def each_window(strips, scalars, first, last, group, found, item):
    start = scalars[0]
    stride = max(4 // len(group), 1)
    turns = (functools.reduce(jnp.maximum, [high - low for low, high in found]) + stride - 1) // stride
    streams = [
        (place * stride + ahead, which, low + ahead, high)
        for place, (which, (low, high)) in enumerate(zip(group, found, strict=True))
        for ahead in range(stride)
    ]

    def one_turn(step, carry):
        more = []
        for place, which, low, high in streams:
            valid = low + step * stride < high
            turn = jnp.minimum(low + step * stride, first.shape[2] - 1)
            at, count = windows(strips, start, first, last, which, turn)
            item(place, which, turn, pl.multiple_of(at, 128), valid)
            more.append((place, which, turn, at, jnp.where(valid, count, 0)))
        for place, which, turn, at, count in more:

            def one_window(extra, carry, place=place, which=which, turn=turn, at=at):
                item(place, which, turn, pl.multiple_of(at + extra * window, 128), True)
                return carry

            lax.fori_loop(1, count, one_window, 0)
        return carry

    lax.fori_loop(0, turns, one_turn, 0)


def values_of(lists, which, what, turn):
    rows = block // 128
    return jnp.concatenate([lists[which, what, pl.ds(turn * rows + i, 1)] for i in range(rows)], 1)


def cells_of(strips, scalars, lists, which, turn, at, valid):
    row = values_of(lists, which, 0, turn).astype(jnp.int32) - at
    row = jnp.where((row >= -1) & (row < window) & valid, row, -10)
    col = values_of(lists, which, 1, turn).astype(jnp.int32) - scalars[0]
    col = jnp.where((col >= 0) & (col < strips), col, -10)
    return (row, col)


def groups_of(count):
    return [tuple(range(first, min(first + 4, count))) for first in range(0, count, 4)]


def deposit_body(strips, scalars, first, last, weights, lists, charge, parts):
    pad_cols = charge.shape[1]
    tall = -(-pad_cols // 16) * 16
    count = lists.shape[0]
    for part in parts:
        part[...] = jnp.zeros_like(part)

    def half_of(which):
        return which // (count // 2)

    def item(place, which, turn, at, valid):
        row, col = cells_of(strips, scalars, lists, which, turn, at, valid)
        amount = values_of(lists, which, 2, turn)
        near, far = (weights[which, 2] * amount, weights[which, 3] * amount)
        near_high, far_high = (near.astype(jnp.bfloat16), far.astype(jnp.bfloat16))
        near_low = (near - near_high.astype(jnp.float32)).astype(jnp.bfloat16)
        far_low = (far - far_high.astype(jnp.float32)).astype(jnp.bfloat16)
        col = short(col)
        cols = jnp.concatenate(
            [pair_weights(col, near_high, far_high, tall), pair_weights(col, near_low, far_low, tall)], 0
        )
        rows = pair_weights(short(row), short(weights[which, 0]), short(weights[which, 1]), window)
        both = dot(cols, rows, ((1,), (1,)))
        half = half_of(which) if count > 4 else 0
        parts[place if count > 4 else half_of(which)][half, :, pl.ds(at, window)] += both[:pad_cols] + both[tall : tall + pad_cols]

    for group in groups_of(count):
        each_window(strips, scalars, first, last, group, strip_blocks(strips, scalars, first, last, group), item)
    for half in range(2):
        if count > 4:
            used = [part[half] for part in parts]
        else:
            used = [parts[half][0]]
        charge[half] = functools.reduce(jnp.add, used)


def deposit_parts(count, charge_shape):
    return [pltpu.VMEM((2 if count > 4 else 1, *charge_shape[1:]), jnp.float32)] * (4 if count > 4 else 2)


def sample_start(strips, scalars, first, last, kicks, begin):
    for kick in kicks:
        kick[...] = jnp.zeros_like(kick)
    groups = [tuple(begin + which for which in group) for group in groups_of(len(kicks))]
    return [(group, strip_blocks(strips, scalars, first, last, group)) for group in groups]


def sample_body(strips, scalars, first, last, weights, lists, field_high, field_low, kicks, begin, started):
    pad_cols = field_high.shape[1] // 2

    def item(place, which, turn, at, valid):
        half = scalars[1 + which]
        kick = kicks[which - begin]
        row, col = cells_of(strips, scalars, lists, which, turn, at, valid)
        rows = pair_weights(short(row), short(weights[which, 0]), short(weights[which, 1]), window)
        fields = jnp.concatenate([field_high[half, :, pl.ds(at, window)], field_low[half, :, pl.ds(at, window)]], 1)
        near = dot(fields, jnp.concatenate([rows, rows], 0), ((1,), (0,)))
        cols = pair_weights(col.astype(jnp.float32), weights[which, 2], weights[which, 3], pad_cols)
        for component, part in enumerate((near[:pad_cols], near[pad_cols:])):
            total = jnp.sum(part * cols, axis=0, keepdims=True)
            for i in range(block // 128):
                kick[component, pl.ds(turn * (block // 128) + i, 1)] += total[:, i * 128 : (i + 1) * 128]

    for group, found in started:
        each_window(strips, scalars, first, last, group, found, item)


def fetch(stored, tables, arrived, parts):
    copies = {part: [] for part in parts}
    for number, (part, piece) in enumerate((part, piece) for part in parts for piece in range(pieces)):
        rows = pl.ds(piece * piece_rows, piece_rows)
        copies[part].append(pltpu.make_async_copy(stored.at[part, rows], tables.at[part, rows], arrived.at[number]))
        copies[part][-1].start()

    def table(part, begin=0, end=pieces):
        for copy in copies[part][begin:end] + copies[part + 1][begin:end]:
            copy.wait()
        rows = slice(begin * piece_rows, end * piece_rows)
        return (tables[part, rows], tables[part + 1, rows])

    return table


def modes_kernel(strips, scalars, first, last, weights, lists, stored, sent_modes, charge, tables, arrived, by_mode, sent, *parts):
    table = fetch(stored, tables, arrived, (0, 1))
    deposit_body(strips, scalars, first, last, weights, lists, charge, parts)
    devices, pad_cols, modes = by_mode.shape
    near, far = (charge[0, :, :HALF], charge[1, :, :HALF])
    high, low = table(0)
    both = jnp.concatenate([(near + far) * alternate((1, HALF), 1), near - far], 0)
    copies = []
    quarter = devices // 4
    for part in range(2):
        done = dot_parts(high[:, part * HALF // 2 : (part + 1) * HALF // 2], low[:, part * HALF // 2 : (part + 1) * HALF // 2], both, ((1,), (0,)))
        for turn in range(quarter):
            here = slice(turn * modes, (turn + 1) * modes)
            by_mode[part * quarter + turn] = done[:pad_cols, here]
            by_mode[devices // 2 + part * quarter + turn] = done[pad_cols:, here]
        for parity in range(2):
            here = pl.ds(parity * (devices // 2) + part * quarter, quarter)
            copies.append(pltpu.make_async_copy(by_mode.at[here], sent_modes.at[here], sent.at[2 * part + parity]))
            copies[-1].start()
    for copy in copies:
        copy.wait()


def columns_kernel(order, flipped, per_tile, strips, by_mode, lam, wave, mine, stored, halves, tables, arrived, outgoing, sent):
    table = fetch(stored, tables, arrived, (0, 1, 2, 3))
    sine_parts = table(0)
    modes = by_mode.shape[2]
    near, far = ([], [])
    for place in range(len(order)):
        pair = []
        for here, before in ((order, 0), (flipped, len(order))):
            body = by_mode[before + here[place], :strips]
            if place % per_tile:
                halo = by_mode[before + here[place - 1], strips:]
                body = jnp.concatenate([body[:8] + halo, body[8:]], 0)
            pair.append(body)
        near.append(pair[0] + pair[1])
        far.append(pair[0] - pair[1])
    columns = jnp.concatenate([jnp.concatenate(near, 0).T * alternate((1, HALF), 1), jnp.concatenate(far, 0).T], 0)
    spectrum = dot_parts(*sine_parts, columns, ((1,), (0,)))
    lam_mine, wave_mine = (mine[:, 0:1], mine[:, 1:2])
    hats = ([], [])
    for parity in range(2):
        this = slice(parity, parity + 1)
        hat = spectrum[parity * modes : (parity + 1) * modes] * (1.0 / (lam[this, :] + lam_mine))
        hats[0].append((hat * wave_mine).T)
        hats[1].append((hat * wave[this, :]).T)

    copies = []
    wide = 2 * strips
    outgoing[:, wide:] = jnp.zeros((outgoing.shape[0], 8, modes), jnp.float32)
    for component, sign in enumerate((1, -1)):
        hat = jnp.concatenate(hats[component], 1)
        hat_high = hat.astype(jnp.bfloat16)
        hat_both = jnp.concatenate([hat_high, (hat - hat_high.astype(jnp.float32)).astype(jnp.bfloat16)], 1)
        parts = sine_parts if component == 0 else table(2)
        for piece in range(pieces):
            high, low = (part[piece * piece_rows : (piece + 1) * piece_rows] for part in parts)
            done = dot(high, hat_both, ((1,), (0,)))
            done = done[:, : 2 * modes] + done[:, 2 * modes :] + dot(low, hat_high, ((1,), (0,)))
            even, odd = (done[:, :modes] * (sign * alternate((piece_rows, modes), 0)), done[:, modes:])
            for before, whose, value in (
                (0, order, even + odd),
                (len(order), flipped, even - odd if sign == 1 else odd - even),
            ):
                for turn in range(piece_rows // strips):
                    place = piece * piece_rows // strips + turn
                    part = value[turn * strips : (turn + 1) * strips]
                    outgoing[before + whose[place], component * strips : (component + 1) * strips] = part
                    if place % per_tile:
                        outgoing[before + whose[place - 1], wide + component : wide + component + 1] = part[:1]
        here = pl.ds(0, strips) if component == 0 else pl.ds(strips, strips + 8)
        copies.append(pltpu.make_async_copy(outgoing.at[:, here], halves.at[:, here], sent.at[component]))
        copies[-1].start()
    for copy in copies:
        copy.wait()


def kicks_kernel(strips, scalars, first, last, weights, lists, halves, stored, *refs):
    kicks, (field_high, field_low, tables, arrived) = (refs[:-4], refs[-4:])
    table = fetch(stored, tables, arrived, (2, 3, 0, 1))
    started = sample_start(strips, scalars, first, last, kicks, 0)
    devices = halves.shape[0]
    pad_cols = strips + 8
    wide = 2 * pad_cols
    fields = {}
    for component, sign in enumerate((-1, 1)):
        sides = []
        for start in (0, devices // 2):
            for here in (slice(component * strips, (component + 1) * strips), slice(2 * strips, 2 * strips + 8)):
                sides.append(jnp.concatenate([halves[start + turn, here] for turn in range(devices // 2)], 1))
            after = jnp.broadcast_to(sides[-1][component : component + 1], sides[-1].shape)
            sides[-1] = jnp.where(lax.broadcasted_iota(jnp.int32, after.shape, 0) == 0, after, 0.0)
        both = jnp.concatenate(sides, 0)
        done = 0.0
        for piece in range(pieces):
            rows = slice(piece * piece_rows, (piece + 1) * piece_rows)
            done += dot_parts(*table(2 - 2 * component, piece, piece + 1), both[:, rows], ((1,), (0,)))
        even, odd = (done[:pad_cols] * (sign * alternate((1, HALF), 1)), done[pad_cols:])
        fields[component] = (even + odd, even - odd if sign == 1 else odd - even)
    for half in range(2):
        value = jnp.concatenate([fields[component][half] for component in range(2)], 0)
        high = value.astype(jnp.bfloat16)
        field_high[half, :, :HALF] = high
        field_low[half, :, :HALF] = (value - high.astype(jnp.float32)).astype(jnp.bfloat16)
        beyond = jnp.zeros((wide, window), jnp.bfloat16)
        field_high[half, :, HALF:] = beyond
        field_low[half, :, HALF:] = beyond
    sample_body(strips, scalars, first, last, weights, lists, field_high, field_low, kicks, 0, started)


def block_ends(lists):
    rows = block // 128
    ends = (lists[:, :2, 0::rows, 0], lists[:, :2, rows - 1 :: rows, 127])
    return tuple(end.astype(jnp.int32) for end in ends)


def deposit_alone(strips, scalars, first, last, weights, lists, charge, *parts):
    deposit_body(strips, scalars, first, last, weights, lists, charge, parts)


def sample_alone(strips, begin, scalars, first, last, weights, lists, field_high, field_low, *kicks):
    started = sample_start(strips, scalars, first, last, kicks, begin)
    sample_body(strips, scalars, first, last, weights, lists, field_high, field_low, kicks, begin, started)


def shifted(n_tx, n_dom, shift):
    return [
        ((a + shift[0]) % n_tx * n_dom + (c + shift[1]) % n_dom, a * n_dom + c) for a in range(n_tx) for c in range(n_dom)
    ]


def returned(route, n_tx, n_dom, shift):
    pairs = []
    for there, here in route:
        for a in range(n_tx):
            for c in range(n_dom):
                target = ((there // 2 * n_tx + (a + shift[0]) % n_tx) * 2 + there % 2) * n_dom + (c + shift[1]) % n_dom
                pairs.append((((here // 2 * n_tx + a) * 2 + here % 2) * n_dom + c, target))
    return pairs


def general(to_deposit, to_sample, tables, lam_e, lam_o, lam_k, sizes, charge_shape, kick_shape):
    n_tx, n_lo, n_dom = sizes
    devices = 2 * n_tx * n_lo * n_dom
    modes = GRID // devices
    tile_cols = HALF // n_lo
    strips = tile_cols // (n_tx * n_dom)
    pad_cols = charge_shape[1]
    smem, vmem = (pl.BlockSpec(memory_space=pltpu.SMEM), pl.BlockSpec(memory_space=pltpu.VMEM))
    params = pltpu.CompilerParams(vmem_limit_bytes=vmem_limit)
    sine_e, sine_o, slope_e, slope_o = tables
    starts = np.array([b * tile_cols + (a * n_dom + c) * strips for a in range(n_tx) for b in range(n_lo) for c in range(n_dom)])
    offsets = np.arange(pad_cols)
    columns = starts[:, None] + offsets
    kept = (offsets <= strips) & (columns < HALF)
    picked = np.where(kept, columns, 0).reshape(-1)
    used = kept.reshape(-1, 1)
    strip_sine_e, strip_sine_o, strip_slope_e, strip_slope_o = (
        tuple(jnp.asarray(part) for part in split_table(table[picked] * used)) for table in basis_tables()
    )

    charge = pl.pallas_call(
        functools.partial(deposit_alone, strips),
        out_shape=jax.ShapeDtypeStruct(charge_shape, jnp.float32),
        in_specs=[smem] * 4 + [vmem],
        out_specs=vmem,
        scratch_shapes=deposit_parts(n_tx * n_dom, charge_shape),
        compiler_params=params,
        name="deposit",
    )(*to_deposit)[:, :, :HALF]

    even = table_right(charge[0] + charge[1], sine_e, 0)
    odd = table_right(charge[0] - charge[1], sine_o, 0)
    by_mode = jnp.concatenate([even, odd], 1).reshape(pad_cols, devices, modes).transpose(1, 0, 2)
    by_mode = lax.all_to_all(by_mode, cube, 0, 0, tiled=True)

    def flip(part):
        return part.reshape(n_tx, n_lo, n_dom, pad_cols, modes)[:, ::-1].reshape(devices // 2, pad_cols, modes)

    near, far = (by_mode[: devices // 2], flip(by_mode[devices // 2 :]))
    folded = (devices // 2 * pad_cols, modes)
    spectrum_e = table_left(strip_sine_e, (near + far).reshape(folded), 0)
    spectrum_o = table_left(strip_sine_o, (near - far).reshape(folded), 0)
    hat_e = spectrum_e * (1.0 / (lam_e[:, None] + lam_k[None, :]))
    hat_o = spectrum_o * (1.0 / (lam_o[:, None] + lam_k[None, :]))
    shape = (devices // 2, pad_cols, modes)
    along_e = table_left(strip_sine_e, hat_e, 1).reshape(shape)
    along_o = table_left(strip_sine_o, hat_o, 1).reshape(shape)
    across_e = table_left(strip_slope_e, hat_e, 1).reshape(shape)
    across_o = table_left(strip_slope_o, hat_o, 1).reshape(shape)
    halves = jnp.concatenate(
        [
            jnp.stack([along_e + along_o, across_e + across_o], 1),
            jnp.stack([flip(along_e - along_o), flip(across_o - across_e)], 1),
        ],
        0,
    )
    halves = lax.all_to_all(halves, cube, 0, 0, tiled=True)

    halves = halves.transpose(1, 2, 0, 3).reshape(2, pad_cols, GRID)
    x_e = table_right(halves[0, :, :HALF], slope_e, 1)
    x_o = table_right(halves[0, :, HALF:], slope_o, 1)
    y_e = table_right(halves[1, :, :HALF], sine_e, 1)
    y_o = table_right(halves[1, :, HALF:], sine_o, 1)
    field = jnp.stack([jnp.concatenate([x_e + x_o, y_e + y_o], 0), jnp.concatenate([x_o - x_e, y_e - y_o], 0)])
    field = jnp.pad(field, ((0, 0), (0, 0), (0, window)))
    field_high, field_low = split(field)

    return pl.pallas_call(
        functools.partial(sample_alone, strips, 0),
        out_shape=[kick_shape] * (n_tx * n_dom),
        in_specs=[smem] * 4 + [vmem] * 3,
        out_specs=[vmem] * (n_tx * n_dom),
        compiler_params=params,
        name="sample",
    )(*to_sample, field_high, field_low)


def shards(cell_row, cell_col, weights, momenta):
    n_tx, n_lo, n_dom = (lax.axis_size(name) for name in ("tx", "lo", "dom"))
    tile_rows = GRID // n_tx
    tile_cols = HALF // n_lo
    lists = n_tx * n_dom
    strips = tile_cols // lists
    pad_cols = strips + 8
    devices = 2 * n_lo * lists
    modes = GRID // devices
    count = cell_row.shape[1]
    q, hi, lo, tx, dom = (lax.axis_index(name) for name in ("q", "hi", "lo", "tx", "dom"))

    row, col = lax.optimization_barrier((cell_row.reshape(-1, 128), cell_col.reshape(-1, 128)))
    amount = weights[0]
    row = jnp.where(tx >= n_tx // 2, (n_tx - 1 - tx) * tile_rows + (tile_rows - 2) - row, tx * tile_rows + row)
    col = jnp.where(hi == 1, tile_cols - 2 - col, col)
    strip_bits = strips.bit_length() - 1
    key = ((lax.shift_right_logical(col, strip_bits) * HALF + row) << strip_bits) + (col & (strips - 1))
    key, amount, order = lax.sort((key.reshape(-1), amount, lax.iota(jnp.int32, count)), num_keys=1, is_stable=False)
    row = lax.shift_right_logical(key, strip_bits) & (HALF - 1)
    col = (key // (strips * HALF) << strip_bits) + (key & (strips - 1))
    row, col, amount = (values.astype(jnp.float32).reshape(-1, 128) for values in (row, col, amount))

    own_route = [(b * 2 + t, t * 2 + b) for b in range(2) for t in range(2)]
    other_route = [(b * 2 + t, t * 2 + 1 - b) for b in range(2) for t in range(2)]
    own = lax.ppermute(jnp.stack([row, col, amount]), ("q", "hi"), own_route)
    mine, own = lax.optimization_barrier((jnp.stack([row, col]), own))
    other = lax.ppermute(mine, ("q", "hi"), other_route)
    own = lax.all_gather(own, ("tx", "dom"), axis=0)
    other, own = lax.optimization_barrier((other, own))
    shifts = [(a, c) for a in range(n_tx) for c in range(n_dom)][::-1]
    others = [lax.ppermute(other, ("tx", "dom"), shifted(n_tx, n_dom, shift)) if any(shift) else other for shift in shifts]
    sources_tx = jnp.stack([(tx + a) % n_tx for a, _ in shifts])

    strip_start = (tx * n_dom + dom) * strips
    col_pair = jnp.where(q == 1, jnp.array([[0.375, 0.625]]), jnp.array([[0.625, 0.375]]))

    def settings(list_tx):
        upper = list_tx >= n_tx // 2
        row_pair = jnp.where(upper[:, None], jnp.array([[0.25, 0.75]]), jnp.array([[0.75, 0.25]]))
        pairs = jnp.concatenate([row_pair, jnp.broadcast_to(col_pair, (lists, 2))], 1).astype(jnp.float32)
        return (jnp.concatenate([strip_start[None], upper]).astype(jnp.int32), pairs)

    own_scalars, own_pairs = settings(jnp.arange(lists) // n_dom)
    other_scalars, other_pairs = settings(sources_tx)
    smem, vmem = (pl.BlockSpec(memory_space=pltpu.SMEM), pl.BlockSpec(memory_space=pltpu.VMEM))
    params = pltpu.CompilerParams(vmem_limit_bytes=vmem_limit)

    to_deposit = (own_scalars, *block_ends(own), own_pairs, own)
    charge_shape = (2, pad_cols, HALF + window)
    kick_shape = jax.ShapeDtypeStruct((2, count // 128, 128), jnp.float32)

    angles = np.pi * (np.arange(GRID) + 1) / (2 * (GRID + 1))
    lam = (4.0 * np.sin(angles) ** 2).astype(np.float32)
    lam_e, lam_o = (lam[0::2], lam[1::2])
    lam_k = lax.dynamic_slice_in_dim(jnp.asarray(np.concatenate([lam_e, lam_o])), lax.axis_index(cube) * modes, modes)

    if modes % 128 == 0 and strips % 8 == 0 and piece_rows % strips == 0:
        stored = jnp.asarray(folded_tables())
        anywhere = pl.BlockSpec(memory_space=pl.ANY)
        fetched = [pltpu.VMEM(stored.shape, stored.dtype), pltpu.SemaphoreType.DMA((4 * pieces,))]
        outgoing = pltpu.VMEM((devices, 2 * strips + 8, modes), jnp.float32)
        by_mode = pl.pallas_call(
            functools.partial(modes_kernel, strips),
            out_shape=jax.ShapeDtypeStruct((devices, pad_cols, modes), jnp.float32),
            in_specs=[smem] * 4 + [vmem, anywhere],
            out_specs=anywhere,
            scratch_shapes=[
                pltpu.VMEM(charge_shape, jnp.float32),
                pltpu.VMEM((2, HALF, HALF), jnp.bfloat16),
                fetched[1],
                pltpu.VMEM((devices, pad_cols, modes), jnp.float32),
                pltpu.SemaphoreType.DMA((4,)),
                *deposit_parts(lists, charge_shape),
            ],
            compiler_params=params,
            name="modes",
        )(*to_deposit, stored)
        by_mode, *others = lax.optimization_barrier((by_mode, *others))
        other = jnp.stack(others)
        by_mode = lax.all_to_all(by_mode, cube, 0, 0, tiled=True)
        order_k = np.concatenate([GRID - 2 - 2 * np.arange(HALF), 2 * np.arange(HALF) + 1])
        wave = (-np.pi * (np.arange(GRID) + 1) / (GRID + 1)).astype(np.float32)
        mine = jnp.asarray(np.stack([lam[order_k], wave[order_k]], 1))
        mine = lax.dynamic_slice_in_dim(mine, lax.axis_index(cube) * modes, modes)
        natural = [(b, a * n_dom + c) for b in range(n_lo) for a in range(n_tx) for c in range(n_dom)]
        straight = [(j // n_dom * n_lo + b) * n_dom + j % n_dom for b, j in natural]
        flipped = [(j // n_dom * n_lo + n_lo - 1 - b) * n_dom + j % n_dom for b, j in natural]
        halves = pl.pallas_call(
            functools.partial(columns_kernel, straight, flipped, lists, strips),
            out_shape=jax.ShapeDtypeStruct(outgoing.shape, jnp.float32),
            in_specs=[vmem] * 4 + [anywhere],
            out_specs=anywhere,
            scratch_shapes=[*fetched, outgoing, pltpu.SemaphoreType.DMA((2,))],
            compiler_params=pltpu.CompilerParams(vmem_limit_bytes=51 * 1024 * 1024),
            name="columns",
        )(by_mode, *(jnp.asarray(values[order_k].reshape(2, HALF)) for values in (lam, wave)), mine, stored)
        halves = lax.all_to_all(halves, cube, 0, 0, tiled=True)
        to_sample = (other_scalars, *block_ends(other), other_pairs, other)
        fields_shape = jax.ShapeDtypeStruct((2, 2 * pad_cols, HALF + window), jnp.bfloat16)
        early = lists // 2
        *kicks, field_high, field_low = pl.pallas_call(
            functools.partial(kicks_kernel, strips),
            out_shape=[kick_shape] * early + [fields_shape] * 2,
            in_specs=[smem] * 4 + [vmem] * 2 + [anywhere],
            out_specs=[vmem] * (early + 2),
            scratch_shapes=fetched,
            compiler_params=params,
            name="kicks",
        )(*to_sample, halves, stored)
        kicks += pl.pallas_call(
            functools.partial(sample_alone, strips, early),
            out_shape=[kick_shape] * (lists - early),
            in_specs=[smem] * 4 + [vmem] * 3,
            out_specs=[vmem] * (lists - early),
            compiler_params=params,
            name="sample",
        )(*to_sample, field_high, field_low)
    else:
        other = jnp.stack(others)
        to_sample = (other_scalars, *block_ends(other), other_pairs, other)
        tables = [tuple(jnp.asarray(part) for part in split_table(table)) for table in basis_tables()]
        kicks = general(to_deposit, to_sample, tables, lam_e, lam_o, lam_k, (n_tx, n_lo, n_dom), charge_shape, kick_shape)
    kicks = [
        lax.ppermute(kick, ("q", "tx", "hi", "dom"), returned(other_route, n_tx, n_dom, shift))
        for kick, shift in zip(kicks, shifts, strict=True)
    ]
    kicks = functools.reduce(jnp.add, kicks)
    _, kick_x, kick_y = lax.sort((order, kicks[0].reshape(-1), kicks[1].reshape(-1)), num_keys=1, is_stable=False)
    return momenta + kick_gain * jnp.stack([kick_x, kick_y])[None]


def solution(mesh):
    n_beam, n_tx, n_ty, n_dom = (mesh.shape[name] for name in ("beam", "tx", "ty", "dom"))
    split_mesh = Mesh(mesh.devices.reshape(n_beam, n_tx, 2, n_ty // 2, n_dom), ("q", "tx", "hi", "lo", "dom"))
    where = ("tx", "hi", "lo", "dom")
    placed = (P("q", where), P("q", where), P("q", where), P("q", None, where))
    return jax.shard_map(
        shards,
        mesh=split_mesh,
        in_specs=placed,
        out_specs=P("q", None, where),
        check_vma=False,
    )
```

```python
import functools

import jax
import jax.numpy as jnp
import ml_dtypes
import numpy as np
from jax import lax
from jax.experimental import pallas as pl
from jax.experimental.pallas import tpu as pltpu
from jax.sharding import Mesh
from jax.sharding import PartitionSpec as P

GRID = 2048
HALF = GRID // 2
kick_gain = 2.0
block = 512
window = 256
pieces = 2
piece_rows = HALF // pieces
cube = ("q", "tx", "lo", "dom")
vmem_limit = 48 * 1024 * 1024


def split_table(values):
    high = values.astype(ml_dtypes.bfloat16)
    low = (values - high.astype(np.float64)).astype(ml_dtypes.bfloat16)
    return (high, low)


@functools.lru_cache(maxsize=None)
def basis_tables():
    points = GRID + 1
    position = np.arange(HALF)[:, None] + 1
    wave = np.arange(GRID)[None, :] + 1
    angles = np.pi * ((position * wave) % (2 * points)) / points
    scaling = np.sqrt(2.0 / points)
    sine = scaling * np.sin(angles)
    slope = -scaling * (np.pi * wave / points) * np.cos(angles)
    return (sine[:, 0::2], sine[:, 1::2], slope[:, 0::2], slope[:, 1::2])


def folded_tables():
    points = GRID + 1
    number = np.arange(HALF) + 1
    angles = 2 * np.pi * (number[:, None] * number[None, :] % points) / points
    scaling = np.sqrt(2.0 / points)
    return np.stack([part for table in (np.sin(angles), np.cos(angles)) for part in split_table(scaling * table)])


def alternate(shape, dim):
    return (1 - 2 * (lax.broadcasted_iota(jnp.int32, shape, dim) % 2)).astype(jnp.float32)


def split(values):
    high = lax.reduce_precision(values, 8, 7)
    return (high.astype(jnp.bfloat16), (values - high).astype(jnp.bfloat16))


def dot(left, right, dims):
    return lax.dot_general(left, right, (dims, ((), ())), preferred_element_type=jnp.float32)


def table_left(table, values, contract):
    high, low = split(values)
    width = values.shape[1]
    both = dot(table[0], jnp.concatenate([high, low], 1), ((contract,), (0,)))
    return both[:, :width] + both[:, width:] + dot(table[1], high, ((contract,), (0,)))


def table_right(values, table, contract):
    high, low = split(values)
    rows = values.shape[0]
    both = dot(jnp.concatenate([high, low], 0), table[0], ((1,), (contract,)))
    return both[:rows] + both[rows:] + dot(high, table[1], ((1,), (contract,)))


def pair_weights(index, first, second, rows):
    shape = (rows, index.shape[1])
    at = lax.broadcasted_iota(jnp.int32, shape, 0).astype(jnp.float32).astype(index.dtype)
    one, zero = (jnp.ones((), index.dtype), jnp.zeros((), first.dtype))
    return jnp.where(at == index, first, jnp.where(at == index + one, second, zero))


def short(values):
    return values.astype(jnp.float32).astype(jnp.bfloat16)


def dot_parts(table_high, table_low, values, dims):
    high = values.astype(jnp.bfloat16).astype(jnp.float32)
    rows = values.shape[0]
    both = dot(jnp.concatenate([high, values - high], 0).astype(jnp.bfloat16), table_high, dims)
    return both[:rows] + both[rows:] + dot(high.astype(jnp.bfloat16), table_low, dims)


def windows(strips, start, first, last, which, turn):
    first_row, first_col = (first[which, 0, turn], first[which, 1, turn])
    last_row, last_col = (last[which, 0, turn], last[which, 1, turn])
    least = jnp.where(first_col >= start, first_row, 0) // 128 * 128
    most = jnp.where(last_col < start + strips, last_row, HALF - 2)
    return (least, (most + 1 - least) // window + 1)


def strip_blocks(strips, scalars, first, last, group):
    start = scalars[0]

    def bounds(turn, found):
        return tuple(
            (
                low + jnp.where(last[which, 1, turn] < start, 1, 0),
                high + jnp.where(first[which, 1, turn] < start + strips, 1, 0),
            )
            for which, (low, high) in zip(group, found, strict=True)
        )

    return lax.fori_loop(0, first.shape[2], bounds, tuple((0, 0) for _ in group), unroll=8)


def each_window(strips, scalars, first, last, group, found, item):
    start = scalars[0]
    stride = max(4 // len(group), 1)
    turns = (functools.reduce(jnp.maximum, [high - low for low, high in found]) + stride - 1) // stride
    streams = [
        (place * stride + ahead, which, low + ahead, high)
        for place, (which, (low, high)) in enumerate(zip(group, found, strict=True))
        for ahead in range(stride)
    ]

    def one_turn(step, carry):
        more = []
        for place, which, low, high in streams:
            valid = low + step * stride < high
            turn = jnp.minimum(low + step * stride, first.shape[2] - 1)
            at, count = windows(strips, start, first, last, which, turn)
            item(place, which, turn, pl.multiple_of(at, 128), valid)
            more.append((place, which, turn, at, jnp.where(valid, count, 0)))
        for place, which, turn, at, count in more:

            def one_window(extra, carry, place=place, which=which, turn=turn, at=at):
                item(place, which, turn, pl.multiple_of(at + extra * window, 128), True)
                return carry

            lax.fori_loop(1, count, one_window, 0)
        return carry

    lax.fori_loop(0, turns, one_turn, 0)


def values_of(lists, which, what, turn):
    rows = block // 128
    return jnp.concatenate([lists[which, what, pl.ds(turn * rows + i, 1)] for i in range(rows)], 1)


def cells_of(strips, scalars, lists, which, turn, at, valid):
    row = values_of(lists, which, 0, turn).astype(jnp.int32) - at
    row = jnp.where((row >= -1) & (row < window) & valid, row, -10)
    col = values_of(lists, which, 1, turn).astype(jnp.int32) - scalars[0]
    col = jnp.where((col >= 0) & (col < strips), col, -10)
    return (row, col)


def groups_of(count):
    return [tuple(range(first, min(first + 4, count))) for first in range(0, count, 4)]


def deposit_body(strips, scalars, first, last, weights, lists, charge, parts):
    pad_cols = charge.shape[1]
    tall = -(-pad_cols // 16) * 16
    count = lists.shape[0]
    for part in parts:
        part[...] = jnp.zeros_like(part)

    def half_of(which):
        return which // (count // 2)

    def item(place, which, turn, at, valid):
        row, col = cells_of(strips, scalars, lists, which, turn, at, valid)
        amount = values_of(lists, which, 2, turn)
        near, far = (weights[which, 2] * amount, weights[which, 3] * amount)
        near_high, far_high = (near.astype(jnp.bfloat16), far.astype(jnp.bfloat16))
        near_low = (near - near_high.astype(jnp.float32)).astype(jnp.bfloat16)
        far_low = (far - far_high.astype(jnp.float32)).astype(jnp.bfloat16)
        col = short(col)
        cols = jnp.concatenate(
            [pair_weights(col, near_high, far_high, tall), pair_weights(col, near_low, far_low, tall)], 0
        )
        rows = pair_weights(short(row), short(weights[which, 0]), short(weights[which, 1]), window)
        both = dot(cols, rows, ((1,), (1,)))
        half = half_of(which) if count > 4 else 0
        parts[place if count > 4 else half_of(which)][half, :, pl.ds(at, window)] += both[:pad_cols] + both[tall : tall + pad_cols]

    for group in groups_of(count):
        each_window(strips, scalars, first, last, group, strip_blocks(strips, scalars, first, last, group), item)
    for half in range(2):
        if count > 4:
            used = [part[half] for part in parts]
        else:
            used = [parts[half][0]]
        charge[half] = functools.reduce(jnp.add, used)


def deposit_parts(count, charge_shape):
    return [pltpu.VMEM((2 if count > 4 else 1, *charge_shape[1:]), jnp.float32)] * (4 if count > 4 else 2)


def sample_start(strips, scalars, first, last, kicks, begin):
    for kick in kicks:
        kick[...] = jnp.zeros_like(kick)
    groups = [tuple(begin + which for which in group) for group in groups_of(len(kicks))]
    return [(group, strip_blocks(strips, scalars, first, last, group)) for group in groups]


def sample_body(strips, scalars, first, last, weights, lists, field_high, field_low, kicks, begin, started):
    pad_cols = field_high.shape[1] // 2

    def item(place, which, turn, at, valid):
        half = scalars[1 + which]
        kick = kicks[which - begin]
        row, col = cells_of(strips, scalars, lists, which, turn, at, valid)
        rows = pair_weights(short(row), short(weights[which, 0]), short(weights[which, 1]), window)
        fields = jnp.concatenate([field_high[half, :, pl.ds(at, window)], field_low[half, :, pl.ds(at, window)]], 1)
        near = dot(fields, jnp.concatenate([rows, rows], 0), ((1,), (0,)))
        cols = pair_weights(col.astype(jnp.float32), weights[which, 2], weights[which, 3], pad_cols)
        for component, part in enumerate((near[:pad_cols], near[pad_cols:])):
            total = jnp.sum(part * cols, axis=0, keepdims=True)
            for i in range(block // 128):
                kick[component, pl.ds(turn * (block // 128) + i, 1)] += total[:, i * 128 : (i + 1) * 128]

    for group, found in started:
        each_window(strips, scalars, first, last, group, found, item)


def fetch(stored, tables, arrived, parts):
    copies = {part: [] for part in parts}
    for number, (part, piece) in enumerate((part, piece) for part in parts for piece in range(pieces)):
        rows = pl.ds(piece * piece_rows, piece_rows)
        copies[part].append(pltpu.make_async_copy(stored.at[part, rows], tables.at[part, rows], arrived.at[number]))
        copies[part][-1].start()

    def table(part, begin=0, end=pieces):
        for copy in copies[part][begin:end] + copies[part + 1][begin:end]:
            copy.wait()
        rows = slice(begin * piece_rows, end * piece_rows)
        return (tables[part, rows], tables[part + 1, rows])

    return table


def modes_kernel(strips, scalars, first, last, weights, lists, stored, sent_modes, charge, tables, arrived, by_mode, sent, *parts):
    table = fetch(stored, tables, arrived, (0, 1))
    deposit_body(strips, scalars, first, last, weights, lists, charge, parts)
    devices, pad_cols, modes = by_mode.shape
    near, far = (charge[0, :, :HALF], charge[1, :, :HALF])
    high, low = table(0)
    both = jnp.concatenate([(near + far) * alternate((1, HALF), 1), near - far], 0)
    copies = []
    quarter = devices // 4
    for part in range(2):
        done = dot_parts(high[:, part * HALF // 2 : (part + 1) * HALF // 2], low[:, part * HALF // 2 : (part + 1) * HALF // 2], both, ((1,), (0,)))
        for turn in range(quarter):
            here = slice(turn * modes, (turn + 1) * modes)
            by_mode[part * quarter + turn] = done[:pad_cols, here]
            by_mode[devices // 2 + part * quarter + turn] = done[pad_cols:, here]
        for parity in range(2):
            here = pl.ds(parity * (devices // 2) + part * quarter, quarter)
            copies.append(pltpu.make_async_copy(by_mode.at[here], sent_modes.at[here], sent.at[2 * part + parity]))
            copies[-1].start()
    for copy in copies:
        copy.wait()


def columns_kernel(order, flipped, per_tile, strips, by_mode, lam, wave, mine, stored, halves, tables, arrived, outgoing, sent):
    table = fetch(stored, tables, arrived, (0, 1, 2, 3))
    modes = by_mode.shape[2]
    near, far = ([], [])
    for place in range(len(order)):
        pair = []
        for here, before in ((order, 0), (flipped, len(order))):
            body = by_mode[before + here[place], :strips]
            if place % per_tile:
                halo = by_mode[before + here[place - 1], strips:]
                body = jnp.concatenate([body[:8] + halo, body[8:]], 0)
            pair.append(body)
        near.append(pair[0] + pair[1])
        far.append(pair[0] - pair[1])
    columns = jnp.concatenate([jnp.concatenate(near, 0).T * alternate((1, HALF), 1), jnp.concatenate(far, 0).T], 0)
    sine_parts = table(0)
    spectrum = dot_parts(*sine_parts, columns, ((1,), (0,)))
    lam_mine, wave_mine = (mine[:, 0:1], mine[:, 1:2])
    hats = ([], [])
    for parity in range(2):
        this = slice(parity, parity + 1)
        hat = spectrum[parity * modes : (parity + 1) * modes] * (1.0 / (lam[this, :] + lam_mine))
        hats[0].append((hat * wave_mine).T)
        hats[1].append((hat * wave[this, :]).T)

    copies = []
    wide = 2 * strips
    outgoing[:, wide:] = jnp.zeros((outgoing.shape[0], 8, modes), jnp.float32)
    for component, sign in enumerate((1, -1)):
        hat = jnp.concatenate(hats[component], 1)
        hat_high = hat.astype(jnp.bfloat16)
        hat_both = jnp.concatenate([hat_high, (hat - hat_high.astype(jnp.float32)).astype(jnp.bfloat16)], 1)
        parts = sine_parts if component == 0 else table(2)
        for piece in range(pieces):
            high, low = (part[piece * piece_rows : (piece + 1) * piece_rows] for part in parts)
            done = dot(high, hat_both, ((1,), (0,)))
            done = done[:, : 2 * modes] + done[:, 2 * modes :] + dot(low, hat_high, ((1,), (0,)))
            even, odd = (done[:, :modes] * (sign * alternate((piece_rows, modes), 0)), done[:, modes:])
            for before, whose, value in (
                (0, order, even + odd),
                (len(order), flipped, even - odd if sign == 1 else odd - even),
            ):
                for turn in range(piece_rows // strips):
                    place = piece * piece_rows // strips + turn
                    part = value[turn * strips : (turn + 1) * strips]
                    outgoing[before + whose[place], component * strips : (component + 1) * strips] = part
                    if place % per_tile:
                        outgoing[before + whose[place - 1], wide + component : wide + component + 1] = part[:1]
        here = pl.ds(0, strips) if component == 0 else pl.ds(strips, strips + 8)
        copies.append(pltpu.make_async_copy(outgoing.at[:, here], halves.at[:, here], sent.at[component]))
        copies[-1].start()
    for copy in copies:
        copy.wait()


def kicks_kernel(strips, scalars, first, last, weights, lists, halves, stored, *refs):
    kicks, (field_high, field_low, tables, arrived) = (refs[:-4], refs[-4:])
    table = fetch(stored, tables, arrived, (2, 3, 0, 1))
    started = sample_start(strips, scalars, first, last, kicks, 0)
    devices = halves.shape[0]
    pad_cols = strips + 8
    wide = 2 * pad_cols
    fields = {}
    for component, sign in enumerate((-1, 1)):
        sides = []
        for start in (0, devices // 2):
            for here in (slice(component * strips, (component + 1) * strips), slice(2 * strips, 2 * strips + 8)):
                sides.append(jnp.concatenate([halves[start + turn, here] for turn in range(devices // 2)], 1))
            after = jnp.broadcast_to(sides[-1][component : component + 1], sides[-1].shape)
            sides[-1] = jnp.where(lax.broadcasted_iota(jnp.int32, after.shape, 0) == 0, after, 0.0)
        both = jnp.concatenate(sides, 0)
        done = 0.0
        for piece in range(pieces):
            rows = slice(piece * piece_rows, (piece + 1) * piece_rows)
            done += dot_parts(*table(2 - 2 * component, piece, piece + 1), both[:, rows], ((1,), (0,)))
        even, odd = (done[:pad_cols] * (sign * alternate((1, HALF), 1)), done[pad_cols:])
        fields[component] = (even + odd, even - odd if sign == 1 else odd - even)
    for half in range(2):
        value = jnp.concatenate([fields[component][half] for component in range(2)], 0)
        high = value.astype(jnp.bfloat16)
        field_high[half, :, :HALF] = high
        field_low[half, :, :HALF] = (value - high.astype(jnp.float32)).astype(jnp.bfloat16)
        beyond = jnp.zeros((wide, window), jnp.bfloat16)
        field_high[half, :, HALF:] = beyond
        field_low[half, :, HALF:] = beyond
    sample_body(strips, scalars, first, last, weights, lists, field_high, field_low, kicks, 0, started)


def block_ends(lists):
    rows = block // 128
    ends = (lists[:, :2, 0::rows, 0], lists[:, :2, rows - 1 :: rows, 127])
    return tuple(end.astype(jnp.int32) for end in ends)


def deposit_alone(strips, scalars, first, last, weights, lists, charge, *parts):
    deposit_body(strips, scalars, first, last, weights, lists, charge, parts)


def sample_alone(strips, begin, scalars, first, last, weights, lists, field_high, field_low, *kicks):
    started = sample_start(strips, scalars, first, last, kicks, begin)
    sample_body(strips, scalars, first, last, weights, lists, field_high, field_low, kicks, begin, started)


def shifted(n_tx, n_dom, shift):
    return [
        ((a + shift[0]) % n_tx * n_dom + (c + shift[1]) % n_dom, a * n_dom + c) for a in range(n_tx) for c in range(n_dom)
    ]


def returned(route, n_tx, n_dom, shift):
    pairs = []
    for there, here in route:
        for a in range(n_tx):
            for c in range(n_dom):
                target = ((there // 2 * n_tx + (a + shift[0]) % n_tx) * 2 + there % 2) * n_dom + (c + shift[1]) % n_dom
                pairs.append((((here // 2 * n_tx + a) * 2 + here % 2) * n_dom + c, target))
    return pairs


def general(to_deposit, to_sample, tables, lam_e, lam_o, lam_k, sizes, charge_shape, kick_shape):
    n_tx, n_lo, n_dom = sizes
    devices = 2 * n_tx * n_lo * n_dom
    modes = GRID // devices
    tile_cols = HALF // n_lo
    strips = tile_cols // (n_tx * n_dom)
    pad_cols = charge_shape[1]
    smem, vmem = (pl.BlockSpec(memory_space=pltpu.SMEM), pl.BlockSpec(memory_space=pltpu.VMEM))
    params = pltpu.CompilerParams(vmem_limit_bytes=vmem_limit)
    sine_e, sine_o, slope_e, slope_o = tables
    starts = np.array([b * tile_cols + (a * n_dom + c) * strips for a in range(n_tx) for b in range(n_lo) for c in range(n_dom)])
    offsets = np.arange(pad_cols)
    columns = starts[:, None] + offsets
    kept = (offsets <= strips) & (columns < HALF)
    picked = np.where(kept, columns, 0).reshape(-1)
    used = kept.reshape(-1, 1)
    strip_sine_e, strip_sine_o, strip_slope_e, strip_slope_o = (
        tuple(jnp.asarray(part) for part in split_table(table[picked] * used)) for table in basis_tables()
    )

    charge = pl.pallas_call(
        functools.partial(deposit_alone, strips),
        out_shape=jax.ShapeDtypeStruct(charge_shape, jnp.float32),
        in_specs=[smem] * 4 + [vmem],
        out_specs=vmem,
        scratch_shapes=deposit_parts(n_tx * n_dom, charge_shape),
        compiler_params=params,
        name="deposit",
    )(*to_deposit)[:, :, :HALF]

    even = table_right(charge[0] + charge[1], sine_e, 0)
    odd = table_right(charge[0] - charge[1], sine_o, 0)
    by_mode = jnp.concatenate([even, odd], 1).reshape(pad_cols, devices, modes).transpose(1, 0, 2)
    by_mode = lax.all_to_all(by_mode, cube, 0, 0, tiled=True)

    def flip(part):
        return part.reshape(n_tx, n_lo, n_dom, pad_cols, modes)[:, ::-1].reshape(devices // 2, pad_cols, modes)

    near, far = (by_mode[: devices // 2], flip(by_mode[devices // 2 :]))
    folded = (devices // 2 * pad_cols, modes)
    spectrum_e = table_left(strip_sine_e, (near + far).reshape(folded), 0)
    spectrum_o = table_left(strip_sine_o, (near - far).reshape(folded), 0)
    hat_e = spectrum_e * (1.0 / (lam_e[:, None] + lam_k[None, :]))
    hat_o = spectrum_o * (1.0 / (lam_o[:, None] + lam_k[None, :]))
    shape = (devices // 2, pad_cols, modes)
    along_e = table_left(strip_sine_e, hat_e, 1).reshape(shape)
    along_o = table_left(strip_sine_o, hat_o, 1).reshape(shape)
    across_e = table_left(strip_slope_e, hat_e, 1).reshape(shape)
    across_o = table_left(strip_slope_o, hat_o, 1).reshape(shape)
    halves = jnp.concatenate(
        [
            jnp.stack([along_e + along_o, across_e + across_o], 1),
            jnp.stack([flip(along_e - along_o), flip(across_o - across_e)], 1),
        ],
        0,
    )
    halves = lax.all_to_all(halves, cube, 0, 0, tiled=True)

    halves = halves.transpose(1, 2, 0, 3).reshape(2, pad_cols, GRID)
    x_e = table_right(halves[0, :, :HALF], slope_e, 1)
    x_o = table_right(halves[0, :, HALF:], slope_o, 1)
    y_e = table_right(halves[1, :, :HALF], sine_e, 1)
    y_o = table_right(halves[1, :, HALF:], sine_o, 1)
    field = jnp.stack([jnp.concatenate([x_e + x_o, y_e + y_o], 0), jnp.concatenate([x_o - x_e, y_e - y_o], 0)])
    field = jnp.pad(field, ((0, 0), (0, 0), (0, window)))
    field_high, field_low = split(field)

    return pl.pallas_call(
        functools.partial(sample_alone, strips, 0),
        out_shape=[kick_shape] * (n_tx * n_dom),
        in_specs=[smem] * 4 + [vmem] * 3,
        out_specs=[vmem] * (n_tx * n_dom),
        compiler_params=params,
        name="sample",
    )(*to_sample, field_high, field_low)


def shards(cell_row, cell_col, weights, momenta):
    n_tx, n_lo, n_dom = (lax.axis_size(name) for name in ("tx", "lo", "dom"))
    tile_rows = GRID // n_tx
    tile_cols = HALF // n_lo
    lists = n_tx * n_dom
    strips = tile_cols // lists
    pad_cols = strips + 8
    devices = 2 * n_lo * lists
    modes = GRID // devices
    count = cell_row.shape[1]
    q, hi, lo, tx, dom = (lax.axis_index(name) for name in ("q", "hi", "lo", "tx", "dom"))

    row, col = lax.optimization_barrier((cell_row.reshape(-1, 128), cell_col.reshape(-1, 128)))
    amount = weights[0]
    row = jnp.where(tx >= n_tx // 2, (n_tx - 1 - tx) * tile_rows + (tile_rows - 2) - row, tx * tile_rows + row)
    col = jnp.where(hi == 1, tile_cols - 2 - col, col)
    strip_bits = strips.bit_length() - 1
    key = ((lax.shift_right_logical(col, strip_bits) * HALF + row) << strip_bits) + (col & (strips - 1))
    key, amount, order = lax.sort((key.reshape(-1), amount, lax.iota(jnp.int32, count)), num_keys=1, is_stable=False)
    row = lax.shift_right_logical(key, strip_bits) & (HALF - 1)
    col = (key // (strips * HALF) << strip_bits) + (key & (strips - 1))
    row, col, amount = (values.astype(jnp.float32).reshape(-1, 128) for values in (row, col, amount))

    own_route = [(b * 2 + t, t * 2 + b) for b in range(2) for t in range(2)]
    other_route = [(b * 2 + t, t * 2 + 1 - b) for b in range(2) for t in range(2)]
    own = lax.ppermute(jnp.stack([row, col, amount]), ("q", "hi"), own_route)
    mine, own = lax.optimization_barrier((jnp.stack([row, col]), own))
    other = lax.ppermute(mine, ("q", "hi"), other_route)
    own = lax.all_gather(own, ("tx", "dom"), axis=0)
    other, own = lax.optimization_barrier((other, own))
    shifts = [(a, c) for a in range(n_tx) for c in range(n_dom)][::-1]
    others = [lax.ppermute(other, ("tx", "dom"), shifted(n_tx, n_dom, shift)) if any(shift) else other for shift in shifts]
    sources_tx = jnp.stack([(tx + a) % n_tx for a, _ in shifts])

    strip_start = (tx * n_dom + dom) * strips
    col_pair = jnp.where(q == 1, jnp.array([[0.375, 0.625]]), jnp.array([[0.625, 0.375]]))

    def settings(list_tx):
        upper = list_tx >= n_tx // 2
        row_pair = jnp.where(upper[:, None], jnp.array([[0.25, 0.75]]), jnp.array([[0.75, 0.25]]))
        pairs = jnp.concatenate([row_pair, jnp.broadcast_to(col_pair, (lists, 2))], 1).astype(jnp.float32)
        return (jnp.concatenate([strip_start[None], upper]).astype(jnp.int32), pairs)

    own_scalars, own_pairs = settings(jnp.arange(lists) // n_dom)
    other_scalars, other_pairs = settings(sources_tx)
    smem, vmem = (pl.BlockSpec(memory_space=pltpu.SMEM), pl.BlockSpec(memory_space=pltpu.VMEM))
    params = pltpu.CompilerParams(vmem_limit_bytes=vmem_limit)

    to_deposit = (own_scalars, *block_ends(own), own_pairs, own)
    charge_shape = (2, pad_cols, HALF + window)
    kick_shape = jax.ShapeDtypeStruct((2, count // 128, 128), jnp.float32)

    angles = np.pi * (np.arange(GRID) + 1) / (2 * (GRID + 1))
    lam = (4.0 * np.sin(angles) ** 2).astype(np.float32)
    lam_e, lam_o = (lam[0::2], lam[1::2])
    lam_k = lax.dynamic_slice_in_dim(jnp.asarray(np.concatenate([lam_e, lam_o])), lax.axis_index(cube) * modes, modes)

    if modes % 128 == 0 and strips % 8 == 0 and piece_rows % strips == 0:
        stored = jnp.asarray(folded_tables())
        anywhere = pl.BlockSpec(memory_space=pl.ANY)
        fetched = [pltpu.VMEM(stored.shape, stored.dtype), pltpu.SemaphoreType.DMA((4 * pieces,))]
        outgoing = pltpu.VMEM((devices, 2 * strips + 8, modes), jnp.float32)
        by_mode = pl.pallas_call(
            functools.partial(modes_kernel, strips),
            out_shape=jax.ShapeDtypeStruct((devices, pad_cols, modes), jnp.float32),
            in_specs=[smem] * 4 + [vmem, anywhere],
            out_specs=anywhere,
            scratch_shapes=[
                pltpu.VMEM(charge_shape, jnp.float32),
                pltpu.VMEM((2, HALF, HALF), jnp.bfloat16),
                fetched[1],
                pltpu.VMEM((devices, pad_cols, modes), jnp.float32),
                pltpu.SemaphoreType.DMA((4,)),
                *deposit_parts(lists, charge_shape),
            ],
            compiler_params=params,
            name="modes",
        )(*to_deposit, stored)
        by_mode, *others = lax.optimization_barrier((by_mode, *others))
        other = jnp.stack(others)
        by_mode = lax.all_to_all(by_mode, cube, 0, 0, tiled=True)
        order_k = np.concatenate([GRID - 2 - 2 * np.arange(HALF), 2 * np.arange(HALF) + 1])
        wave = (-np.pi * (np.arange(GRID) + 1) / (GRID + 1)).astype(np.float32)
        mine = jnp.asarray(np.stack([lam[order_k], wave[order_k]], 1))
        mine = lax.dynamic_slice_in_dim(mine, lax.axis_index(cube) * modes, modes)
        natural = [(b, a * n_dom + c) for b in range(n_lo) for a in range(n_tx) for c in range(n_dom)]
        straight = [(j // n_dom * n_lo + b) * n_dom + j % n_dom for b, j in natural]
        flipped = [(j // n_dom * n_lo + n_lo - 1 - b) * n_dom + j % n_dom for b, j in natural]
        halves = pl.pallas_call(
            functools.partial(columns_kernel, straight, flipped, lists, strips),
            out_shape=jax.ShapeDtypeStruct(outgoing.shape, jnp.float32),
            in_specs=[vmem] * 4 + [anywhere],
            out_specs=anywhere,
            scratch_shapes=[*fetched, outgoing, pltpu.SemaphoreType.DMA((2,))],
            compiler_params=pltpu.CompilerParams(vmem_limit_bytes=51 * 1024 * 1024),
            name="columns",
        )(by_mode, *(jnp.asarray(values[order_k].reshape(2, HALF)) for values in (lam, wave)), mine, stored)
        halves = lax.all_to_all(halves, cube, 0, 0, tiled=True)
        to_sample = (other_scalars, *block_ends(other), other_pairs, other)
        fields_shape = jax.ShapeDtypeStruct((2, 2 * pad_cols, HALF + window), jnp.bfloat16)
        early = lists // 2
        *kicks, field_high, field_low = pl.pallas_call(
            functools.partial(kicks_kernel, strips),
            out_shape=[kick_shape] * early + [fields_shape] * 2,
            in_specs=[smem] * 4 + [vmem] * 2 + [anywhere],
            out_specs=[vmem] * (early + 2),
            scratch_shapes=fetched,
            compiler_params=params,
            name="kicks",
        )(*to_sample, halves, stored)
        kicks += pl.pallas_call(
            functools.partial(sample_alone, strips, early),
            out_shape=[kick_shape] * (lists - early),
            in_specs=[smem] * 4 + [vmem] * 3,
            out_specs=[vmem] * (lists - early),
            compiler_params=params,
            name="sample",
        )(*to_sample, field_high, field_low)
    else:
        other = jnp.stack(others)
        to_sample = (other_scalars, *block_ends(other), other_pairs, other)
        tables = [tuple(jnp.asarray(part) for part in split_table(table)) for table in basis_tables()]
        kicks = general(to_deposit, to_sample, tables, lam_e, lam_o, lam_k, (n_tx, n_lo, n_dom), charge_shape, kick_shape)
    kicks = [
        lax.ppermute(kick, ("q", "tx", "hi", "dom"), returned(other_route, n_tx, n_dom, shift))
        for kick, shift in zip(kicks, shifts, strict=True)
    ]
    kicks = functools.reduce(jnp.add, kicks)
    _, kick_x, kick_y = lax.sort((order, kicks[0].reshape(-1), kicks[1].reshape(-1)), num_keys=1, is_stable=False)
    return momenta + kick_gain * jnp.stack([kick_x, kick_y])[None]


def solution(mesh):
    n_beam, n_tx, n_ty, n_dom = (mesh.shape[name] for name in ("beam", "tx", "ty", "dom"))
    split_mesh = Mesh(mesh.devices.reshape(n_beam, n_tx, 2, n_ty // 2, n_dom), ("q", "tx", "hi", "lo", "dom"))
    where = ("tx", "hi", "lo", "dom")
    placed = (P("q", where), P("q", where), P("q", where), P("q", None, where))
    return jax.shard_map(
        shards,
        mesh=split_mesh,
        in_specs=placed,
        out_specs=P("q", None, where),
        check_vma=False,
    )
```
